128 devices in a mesh: gx: 16 (over z, x), gy: 8 (over y, core).
Axes of the slice: x: 4, y: 4, z: 4, core: 2. Of those that a mesh axis runs over, the one named last changes fastest.
Arguments:
- load_jump: float32 [16, 8, 2, 512, 256], P('gx', 'gy'), may hold values from -40 to 40
- flex: bfloat16 [16, 8, 2048, 2048], P('gx', 'gy'), may hold values from -1 to 6, as said below
- precond: bfloat16 [16, 8, 2048, 2048], P('gx', 'gy'), may hold values from -1 to 6, as said below
- couple: bfloat16 [16, 8, 8, 2048], P('gx', 'gy'), may hold values from -0.5 to 0.5
- edge_map: int32 [16, 8, 2048], P('gx', 'gy'), may hold values from 0 to 2047, each once within a row
- flags: int32 [16, 8, 2, 512], P('gx', 'gy'), may hold values 0 or 1
- corner_map: int32 [16, 8, 8], replicated, may hold values from 0 to 305, as said below
- coarse_factor: float32 [306, 306], replicated, may hold values from -1 to 2, as said below
Outputs:
- multipliers: float32 [16, 8, 2, 512, 256], P('gx', 'gy')
- residual: float32 [16, 8, 2, 512, 256], P('gx', 'gy')
- direction: float32 [16, 8, 2, 512, 256], P('gx', 'gy')
The draws below stay inside these ranges and needn't reach their ends.
Inputs may be any that keep to these rules, and one draw needn't show every extreme that they name: `corner_map`: subdomain (i, j) has the cross points (i, j), (i+1, j), (i, j+1), (i+1, j+1) of a grid of (17) x (9) cross points as its corners, two fields each, in the order of its eight entries: corner (south-west, south-east, north-west, north-east) times 2 plus field; neighbouring subdomains share cross points; the numbering of the coarse unknowns is a permutation. `flex`: each subdomain's block is symmetric positive definite. `precond`: each subdomain's block is symmetric positive definite. `coarse_factor`: lower triangular with a positive diagonal.
All inputs are finite; a program needn't handle non-finite values. No bound on the sum of `flags` on one device may be relied on, other than what follows from the above.
Results may differ from the reference program's by a relative error of at most 0.01.
The reference program's roundings to bfloat16 on the way (of `spread`) count: a program that leaves them out, or rounds other values in their place, can miss the bound.
Values may be sent and summed in bfloat16 or wider, within the bound.
No kernel may reach another device: no remote copies, remote signals or barrier semaphores. Data moves between devices by JAX's collectives and lax.ppermute only.
A program may use at most 128 MiB of HBM per device.

```python
import math
import jax
import jax.numpy as jnp
from jax import lax

NI = 2048
EW = 512
CASES = 256
ITERS = 2
SDX = 16
SDY = 8
NCO = 306


def assemble_block(noise, diagonal):
    sigma = 0.4 / math.sqrt(2.0 * NI)
    symmetric = (noise + jnp.swapaxes(noise, -1, -2)) * sigma
    positions = lax.iota(jnp.int32, NI)
    identity = (positions[:, None] == positions[None, :]).astype(jnp.float32)
    return symmetric + diagonal[..., None] * identity


def draw_load_jump(key, part):
    key = jax.random.fold_in(key, 1)
    base_key, rough_key = jax.random.split(key, 2)
    shape = (SDX, SDY, 2, NI // 4, CASES)
    flat = lax.iota(jnp.int32, SDX * SDY).astype(jnp.float32).reshape(SDX, SDY, 1, 1, 1)
    ramp = jnp.exp(math.log(3.0) * flat / max(SDX * SDY - 1, 1))
    rough = jnp.exp(jax.random.uniform(rough_key, (SDX, SDY, 2, NI // 4, 1), jnp.float32, math.log(0.3), math.log(3.0)))
    base = jnp.clip(jax.random.normal(base_key, shape, jnp.float32), -4.0, 4.0)
    return jnp.clip(base * rough * ramp, -40.0, 40.0)


def draw_flex(key, part):
    key = jax.random.fold_in(key, 2)
    noise_key, diagonal_key = jax.random.split(key)
    noise = jnp.clip(jax.random.normal(noise_key, (SDX, SDY, NI, NI), jnp.float32), -4.0, 4.0)
    diagonal = jnp.exp(jax.random.uniform(diagonal_key, (SDX, SDY, NI), jnp.float32, 0.0, 1.1))
    return assemble_block(noise, diagonal).astype(jnp.bfloat16)


def draw_precond(key, part):
    key = jax.random.fold_in(key, 3)
    noise_key, diagonal_key = jax.random.split(key)
    noise = jnp.clip(jax.random.normal(noise_key, (SDX, SDY, NI, NI), jnp.float32), -4.0, 4.0)
    diagonal = jnp.exp(jax.random.uniform(diagonal_key, (SDX, SDY, NI), jnp.float32, 0.0, 1.1))
    return assemble_block(noise, diagonal).astype(jnp.bfloat16)


def draw_corner_map(key, part):
    key = jax.random.fold_in(key, 4)
    labels = jax.random.permutation(key, NCO).astype(jnp.int32)
    column_ids = lax.iota(jnp.int32, SDX)[:, None, None]
    row_ids = lax.iota(jnp.int32, SDY)[None, :, None]
    entries = lax.iota(jnp.int32, 8)[None, None, :]
    corner_ids = entries // 2
    field_ids = entries % 2
    cross = (column_ids + corner_ids % 2) * (SDY + 1) + (row_ids + corner_ids // 2)
    return labels[cross * 2 + field_ids].astype(jnp.int32)


def draw_coarse_factor(key, part):
    key = jax.random.fold_in(key, 5)
    noise_key, diagonal_key = jax.random.split(key)
    noise = jnp.clip(jax.random.normal(noise_key, (NCO, NCO), jnp.float32), -4.0, 4.0)
    noise = noise * (0.25 / math.sqrt(NCO))
    positions = lax.iota(jnp.int32, NCO)
    lower = jnp.where(positions[:, None] > positions[None, :], noise, 0.0)
    diagonal = jnp.exp(jax.random.uniform(diagonal_key, (NCO,), jnp.float32, 0.0, math.log(2.0)))
    identity = (positions[:, None] == positions[None, :]).astype(jnp.float32)
    return lower + diagonal[:, None] * identity


def plant(values, own_key, low, high):
    shape = values.shape
    index_at = [jax.random.randint(jax.random.fold_in(own_key, axis), (), 0, shape[axis]) for axis in range(len(shape))]
    values = values.at[tuple(index_at)].set(low)
    longest = shape.index(max(shape))
    index_at[longest] = (index_at[longest] + 1) % shape[longest]
    return values.at[tuple(index_at)].set(high)


def levels(rng, shape, shards, smallest, high):
    loudness = 1.0
    for axis_at, parts in shards:
        draws = jax.random.uniform(jax.random.fold_in(jax.random.fold_in(rng, 6), axis_at), (parts,), jnp.float32, smallest / len(shards), high / len(shards))
        loudness = loudness * jnp.repeat(jnp.exp(draws), shape[axis_at] // parts).reshape((-1,) + (1,) * (len(shape) - 1 - axis_at))
    return loudness


def gaussian(stream_key, dims, scale, bound, cuts=(), held_as=jnp.bfloat16):
    values = scale * jax.random.normal(stream_key, dims, jnp.float32)
    if cuts:
        values = values * levels(stream_key, dims, cuts, -0.22, 0.18)
    return jnp.clip(values, -bound, bound).astype(held_as)


def setup_inputs(seed: int = 0) -> dict:
    key_list = jax.random.split(jax.random.key(seed), 9)
    return {
        "load_jump": draw_load_jump(jax.random.fold_in(key_list[8], 71), 0),
        "flex": draw_flex(jax.random.fold_in(key_list[8], 71), 0),
        "precond": draw_precond(jax.random.fold_in(key_list[8], 71), 0),
        "couple": gaussian(key_list[3], (SDX, SDY, 8, NI), (NI // 16) ** -0.5, 0.5, ((0, 16), (1, 8))),
        "edge_map": jax.vmap(lambda own: jax.random.permutation(own, NI))(jax.random.split(key_list[4], SDX * SDY)).reshape((SDX, SDY, NI)).astype(jnp.int32),
        "flags": plant((jax.random.randint(key_list[5], (SDX, SDY, 2, EW), 0, 8) < 7).astype(jnp.int32), jax.random.fold_in(key_list[5], 1), 0, 1),
        "corner_map": draw_corner_map(jax.random.fold_in(key_list[8], 71), 0),
        "coarse_factor": draw_coarse_factor(jax.random.fold_in(key_list[8], 71), 0),
    }


def spread_edges(values):
    eastern = values[:, :, 0]
    northern = values[:, :, 1]
    western = -jnp.concatenate([jnp.zeros_like(eastern[:1]), eastern[:-1]], axis=0)
    southern = -jnp.concatenate([jnp.zeros_like(northern[:, :1]), northern[:, :-1]], axis=1)
    return jnp.concatenate([western, eastern, southern, northern], axis=2)

def edge_jumps(sides, live_mask):
    width_edge = sides.shape[2] // 4
    western = sides[:, :, :width_edge]
    eastern = sides[:, :, width_edge:2 * width_edge]
    southern = sides[:, :, 2 * width_edge:3 * width_edge]
    northern = sides[:, :, 3 * width_edge:]
    from_east = jnp.concatenate([western[1:], jnp.zeros_like(western[:1])], axis=0)
    from_north = jnp.concatenate([southern[:, 1:], jnp.zeros_like(southern[:, :1])], axis=1)
    return jnp.stack([eastern - from_east, northern - from_north], axis=2) * live_mask

def flatten_pair(matrices, edge_map, values):
    return (matrices.reshape((-1,) + matrices.shape[2:]), edge_map.reshape(-1, edge_map.shape[2]), values.reshape((-1,) + values.shape[2:]))

def block_products(matrices, edge_map, spread):

    def single(operands):
        matrix, order, vector = operands
        placed = jnp.zeros_like(vector).at[order].set(vector)
        return jnp.dot(matrix.astype(jnp.float32), placed.astype(jnp.float32), preferred_element_type=jnp.float32)[order]
    return lax.map(single, flatten_pair(matrices, edge_map, spread)).reshape(spread.shape)

def corner_products(couple, edge_map, spread):

    def single(operands):
        matrix, order, vector = operands
        placed = jnp.zeros_like(vector).at[order].set(vector)
        return jnp.dot(matrix.astype(jnp.float32), placed.astype(jnp.float32), preferred_element_type=jnp.float32)
    result = lax.map(single, flatten_pair(couple, edge_map, spread))
    return result.reshape(spread.shape[:2] + result.shape[1:])

def back_products(couple, edge_map, own_solved):

    def single(operands):
        matrix, order, vector = operands
        return jnp.dot(matrix.astype(jnp.float32).T, vector, precision=lax.Precision.HIGHEST)[order]
    result = lax.map(single, flatten_pair(couple, edge_map, own_solved))
    return result.reshape(own_solved.shape[:2] + result.shape[1:])

def reference(load_jump, flex, precond, couple, edge_map, flags, corner_map, coarse_factor):
    inside_x = jnp.broadcast_to((jnp.arange(SDX) < SDX - 1)[:, None], (SDX, SDY))
    inside_y = jnp.broadcast_to((jnp.arange(SDY) < SDY - 1)[None, :], (SDX, SDY))
    inside = jnp.stack([inside_x, inside_y], axis=2).astype(jnp.float32)
    live_mask = (flags.astype(jnp.float32) * inside[..., None])[..., None]

    def smooth(residual):
        spread = spread_edges((0.5 * residual).astype(jnp.bfloat16))
        return 0.5 * edge_jumps(block_products(precond, edge_map, spread), live_mask)

    def apply_operator(direction):
        spread = spread_edges(direction.astype(jnp.bfloat16))
        local_part = block_products(flex, edge_map, spread)
        corner_terms = corner_products(couple, edge_map, spread)
        coarse_rhs = jax.ops.segment_sum(corner_terms.reshape(-1, CASES), corner_map.reshape(-1), num_segments=NCO)
        solved = jax.scipy.linalg.cho_solve((coarse_factor, True), coarse_rhs)
        own_solved = solved[corner_map]
        sides = local_part + back_products(couple, edge_map, own_solved)
        curvature = jnp.sum(spread.astype(jnp.float32) * sides, axis=(0, 1, 2))
        return (edge_jumps(sides, live_mask), curvature)
    residual = live_mask * load_jump
    smoothed = smooth(residual)
    direction = smoothed
    aligned = jnp.sum(residual * smoothed, axis=(0, 1, 2, 3))
    multipliers = jnp.zeros_like(residual)
    for iteration in range(ITERS):
        image, curvature = apply_operator(direction)
        step_size = aligned / curvature
        multipliers = multipliers + step_size * direction
        residual = residual - step_size * image
        smoothed = smooth(residual)
        aligned_next = jnp.sum(residual * smoothed, axis=(0, 1, 2, 3))
        direction = smoothed + aligned_next / aligned * direction
        aligned = aligned_next
    return (multipliers, residual, direction)
```

```python
import functools

import jax
import jax.numpy as jnp
from jax import lax
from jax.experimental import pallas as pl
from jax.experimental.pallas import tpu as pltpu
from jax.sharding import PartitionSpec as P

ITERS = 2
HIGHEST = lax.Precision.HIGHEST
LANES = 128
CORNER_ROWS = 8
SUMS = 8


def shift(shard, axis, by):
    devices = lax.axis_size(axis)
    pairs = [(i, i + by) for i in range(devices) if 0 <= i + by < devices]
    return lax.ppermute(shard, axis, pairs)


def exchange(west, east, south, north):
    return shift(east, "gx", 1), shift(west, "gx", -1), shift(north, "gy", 1), shift(south, "gy", -1)


def swap(copies, axis):
    return lax.all_to_all(copies, axis, 0, 0, tiled=True)


def call(kernel, out_shape, operands, scratch_shapes=(), in_hbm=(), flops=0, limit=32):
    vmem = pl.BlockSpec(memory_space=pltpu.VMEM)
    specs = [
        pl.BlockSpec(memory_space=pl.ANY) if at in in_hbm else vmem for at in range(len(operands))
    ]
    moved = sum(a.size * a.dtype.itemsize for a in operands)
    return pl.pallas_call(
        kernel,
        out_shape=out_shape,
        in_specs=specs,
        out_specs=jax.tree.map(lambda _: vmem, out_shape),
        scratch_shapes=list(scratch_shapes),
        compiler_params=pltpu.CompilerParams(vmem_limit_bytes=limit * 2**20),
        cost_estimate=pl.CostEstimate(flops=flops, bytes_accessed=moved, transcendentals=0),
    )(*operands)


def shaped(*shape, dtype=jnp.float32):
    return jax.ShapeDtypeStruct(shape, dtype)


def sum_rows(values):
    return jnp.sum(values, axis=0, keepdims=True)


def block_scratch(count, cases):
    tile = min(512, count)
    return [
        pltpu.VMEM((count, count), jnp.bfloat16),
        pltpu.VMEM((count, cases), jnp.bfloat16),
        pltpu.VMEM((count, cases), jnp.bfloat16),
        pltpu.VMEM((count, 2 * cases), jnp.bfloat16),
        pltpu.SemaphoreType.DMA((count // tile,)),
    ]


class Block:
    def __init__(self, matrix_hbm, row_order, column_order, scratch):
        self.matrix_hbm = matrix_hbm
        self.row_order = row_order
        self.column_order = column_order
        self.matrix, self.spread, self.placed, self.parts, self.sems = scratch
        self.count, self.cases = self.spread.shape
        self.tile = min(512, self.count)
        self.tiles = self.count // self.tile

    def rows(self, t):
        return pl.ds(pl.multiple_of(t * self.tile, self.tile), self.tile)

    def fetch(self, t):
        rows = self.rows(t)
        return pltpu.make_async_copy(self.matrix_hbm.at[rows], self.matrix.at[rows], self.sems.at[t])

    def start(self):
        @pl.loop(0, self.tiles)
        def _(t):
            self.fetch(t).start()

    def place(self):
        @pl.loop(0, self.tiles)
        def _(t):
            level = lax.broadcasted_iota(jnp.int32, (self.tile, self.count), 0) + t * self.tile
            select = (level == self.row_order[...]).astype(jnp.bfloat16)
            self.placed[self.rows(t), :] = jnp.dot(
                select, self.spread[...], preferred_element_type=jnp.float32
            ).astype(jnp.bfloat16)

    def multiply(self):
        @pl.loop(0, self.tiles)
        def _(t):
            self.fetch(t).wait()
            product = jnp.dot(
                self.matrix[self.rows(t), :], self.placed[...], preferred_element_type=jnp.float32
            )
            high = product.astype(jnp.bfloat16)
            self.parts[self.rows(t), : self.cases] = high
            self.parts[self.rows(t), self.cases :] = (product - high.astype(jnp.float32)).astype(jnp.bfloat16)

    def back(self, edge):
        level = lax.broadcasted_iota(jnp.int32, (self.count // 4, self.count), 1)
        order = self.column_order[pl.ds(edge * (self.count // 4), self.count // 4), :]
        select = (level == order).astype(jnp.bfloat16)
        both = jnp.dot(select, self.parts[...], preferred_element_type=jnp.float32)
        return both[:, : self.cases] + both[:, self.cases :]


def invert(factor, inverse):
    size = factor.shape[0]
    row = lax.broadcasted_iota(jnp.int32, (LANES, LANES), 0)
    column = lax.broadcasted_iota(jnp.int32, (LANES, LANES), 1)
    blocks = [pl.ds(at, LANES) for at in range(0, size, LANES)]

    def times(left, right):
        return jnp.dot(left, right, precision=HIGHEST, preferred_element_type=jnp.float32)

    inverse[...] = jnp.zeros((size, size), jnp.float32)
    corners = [factor[at, at] for at in blocks]
    solved = [jnp.where(row == column, 1.0 / corner, 0.0) for corner in corners]
    width = 1
    while width < LANES:
        joins = (row // (2 * width) == column // (2 * width)) & (row // width > column // width)
        half = [times(jnp.where(joins, c, 0.0), s) for c, s in zip(corners, solved)]
        solved = [s - times(s, h) for s, h in zip(solved, half)]
        width *= 2
    for n, at in enumerate(blocks):
        if n:
            before = pl.ds(0, n * LANES)
            inverse[at, before] = -times(solved[n], times(factor[at, before], inverse[before, before]))
        inverse[at, at] = solved[n]


def prepare_kernel(factor, piece_labels, corner_labels, couple, row_order, forward, backward, back, inverse):
    invert(factor, inverse)
    size, pieces = forward.shape
    level = lax.broadcasted_iota(jnp.int32, (size, pieces), 0)
    select = (level == piece_labels[...]).astype(jnp.float32)
    forward[...] = jnp.dot(inverse[...], select, precision=HIGHEST, preferred_element_type=jnp.float32)
    level = lax.broadcasted_iota(jnp.int32, backward.shape, 1)
    select = (level == corner_labels[...]).astype(jnp.float32)
    backward[...] = lax.dot_general(
        select, inverse[...], (((1,), (1,)), ((), ())), precision=HIGHEST, preferred_element_type=jnp.float32
    )
    count = couple.shape[1]
    tile = min(512, count)

    @pl.loop(0, count // tile)
    def _(t):
        at = pl.ds(pl.multiple_of(t * tile, tile), tile)
        level = lax.broadcasted_iota(jnp.int32, (count, tile), 0)
        select = (level == row_order[:, at]).astype(jnp.bfloat16)
        back[:, at] = jnp.dot(couple[...], select, preferred_element_type=jnp.float32)


def write_messages(block, messages, back, mask):
    width = block.count // 4
    cut = width // block.cases if width >= block.cases else 1
    for edge, message in enumerate(messages):
        message[pl.ds(0, width), :] = block.back(edge)
        for part in range(cut):
            at = pl.ds(edge * width + part * block.cases, min(block.cases, width))
            message[pl.ds(width + part * CORNER_ROWS, CORNER_ROWS), :] = back[:, at] * mask[:, at]


def smooth_kernel(
    west, east, south, north, row_order, column_order, back, mask, matrix_hbm,
    residual, west_out, east_out, south_out, north_out, total, *scratch,
):
    block = Block(matrix_hbm, row_order, column_order, scratch)
    block.start()
    width = block.count // 4
    for edge, (source, sign) in enumerate(((west, -1.0), (east, 1.0), (south, -1.0), (north, 1.0))):
        at = pl.ds(edge * width, width)
        residual[at, :] = sign * source[pl.ds(0, width), :]
        block.spread[at, :] = (0.5 * residual[at, :]).astype(jnp.bfloat16)
    block.place()
    block.multiply()
    messages = (west_out, east_out, south_out, north_out)
    write_messages(block, messages, back, mask)
    partial = sum(
        sum_rows(residual[pl.ds(edge * width, width), :] * message[pl.ds(0, width), :])
        for edge, message in enumerate(messages)
    )
    total[...] = jnp.broadcast_to(0.5 * partial, total.shape)


def apply_kernel(first, *refs):
    own, refs = refs[:4], refs[4:]
    received, refs = refs[:4], refs[4:]
    if first:
        (total,), refs = refs[:1], refs[1:]
    else:
        (old_direction, pieces, old_aligned), refs = refs[:3], refs[3:]
    row_order, column_order, couple, matrix_hbm = refs[:4]
    direction, refs = refs[4], refs[5:]
    out, refs = refs[:4], refs[4:]
    copies, other = refs[:2]
    block = Block(matrix_hbm, row_order, column_order, refs[2:])
    block.start()
    count, cases = block.count, block.cases
    width = count // 4
    if not first:
        aligned = sum(pieces[device, 0:1, :] for device in range(pieces.shape[0]))
        ratio = aligned / old_aligned[0:1, :]
        other[...] = jnp.broadcast_to(aligned, other.shape)
    for edge in range(4):
        at = pl.ds(edge * width, width)
        smoothed = 0.5 * (own[edge][pl.ds(0, width), :] - received[edge][pl.ds(0, width), :])
        if not first:
            smoothed = smoothed + ratio * old_direction[at, :]
        direction[at, :] = smoothed
        block.spread[at, :] = smoothed.astype(jnp.bfloat16)
    block.place()
    block.multiply()
    curvature = jnp.zeros((1, cases), jnp.float32)
    for edge in range(4):
        at = pl.ds(edge * width, width)
        out[edge][...] = block.back(edge)
        curvature += sum_rows(block.spread[at, :].astype(jnp.float32) * out[edge][...])
    terms = jnp.dot(couple[...], block.placed[...], preferred_element_type=jnp.float32)
    row = lax.broadcasted_iota(jnp.int32, (SUMS, cases), 0)
    sums = jnp.where(row == 0, curvature, 0.0)
    if first:
        sums = sums + jnp.where(row == 1, total[0:1, :], 0.0)
        cut = max(width // cases, 1)
        span = min(width, cases)
        for edge in range(4):
            for part in range(cut):
                at = pl.ds(edge * width + part * span, span)
                rows = pl.ds(width + part * CORNER_ROWS, CORNER_ROWS)
                other[pl.ds(0, CORNER_ROWS), at] = own[edge][rows, :]
                other[pl.ds(CORNER_ROWS, CORNER_ROWS), at] = -received[edge][rows, :]
    for device in range(copies.shape[0]):
        copies[device, pl.ds(0, CORNER_ROWS), :] = terms
        copies[device, pl.ds(CORNER_ROWS, SUMS), :] = sums


def strip_kernel(pieces, copies):
    devices, piece, cases = pieces.shape
    rows = copies.shape[1]
    half = 2 * (devices + 1)
    row = lax.broadcasted_iota(jnp.int32, (rows, devices * piece), 0)
    source = lax.broadcasted_iota(jnp.int32, (rows, devices * piece), 1)
    device, term = source // piece, source % piece
    target = (term // 2) % 2 * half + (device + term // 4) * 2 + term % 2
    target = jnp.where(term < CORNER_ROWS, target, 2 * half + term - CORNER_ROWS)
    select = (row == target).astype(jnp.float32)
    strip = jnp.dot(
        select,
        pieces[...].reshape(devices * piece, cases),
        precision=HIGHEST,
        preferred_element_type=jnp.float32,
    )
    for device in range(copies.shape[0]):
        copies[device] = strip


def update_kernel(first, last, *refs):
    pieces, forward, backward, edge_couple, direction, residual_in = refs[:6]
    own, refs = refs[6:10], refs[10:]
    received, refs = refs[:4], refs[4:]
    if not first:
        (multipliers_in, old_aligned), refs = refs[:2], refs[2:]
    row_order, column_order, matrix_hbm = refs[:3]
    residual, multipliers = refs[3:5]
    out, refs = refs[5:9], refs[9:]
    copies = refs[0]
    if first:
        aligned_out, refs = refs[1], refs[2:]
    else:
        refs = refs[1:]
    kept, *scratch = refs
    block = Block(matrix_hbm, row_order, column_order, scratch)
    block.start()
    count, cases = block.count, block.cases
    width = count // 4
    devices, piece, _ = pieces.shape
    scalar_row = piece - SUMS // 2
    sums = sum(pieces[device, pl.ds(scalar_row, SUMS // 2), :] for device in range(devices))
    half_solved = jnp.dot(
        forward[...],
        pieces[...].reshape(devices * piece, cases),
        precision=HIGHEST,
        preferred_element_type=jnp.float32,
    )
    corners = jnp.dot(backward[...], half_solved, precision=HIGHEST, preferred_element_type=jnp.float32)
    curvature = sums[0:1, :] + sum_rows(half_solved * half_solved)
    if first:
        aligned = sums[1:2, :]
        aligned_out[...] = jnp.broadcast_to(aligned, aligned_out.shape)
    else:
        aligned = old_aligned[0:1, :]
    step_size = aligned / curvature
    for edge in range(4):
        at = pl.ds(edge * width, width)
        beyond = pl.ds((edge + 1) * CORNER_ROWS, CORNER_ROWS)
        solved = jnp.concatenate(
            [corners[0:CORNER_ROWS], corners[(edge + 1) * CORNER_ROWS : (edge + 2) * CORNER_ROWS]]
        )
        high = solved.astype(jnp.bfloat16)
        rest = solved - high.astype(jnp.float32)
        middle = rest.astype(jnp.bfloat16)
        low = (rest - middle.astype(jnp.float32)).astype(jnp.bfloat16)
        coupling = edge_couple[:, at].astype(jnp.bfloat16)
        coarse = lax.dot_general(
            jnp.concatenate([coupling] * 3),
            jnp.concatenate([high, middle, low]),
            (((0,), (0,)), ((), ())),
            preferred_element_type=jnp.float32,
        )
        image = own[edge][...] - received[edge][...] + coarse
        updated = residual_in[at, :] - step_size * image
        block.spread[at, :] = (0.5 * updated).astype(jnp.bfloat16)
        if last:
            kept[at, :] = updated
            if edge % 2:
                residual[edge // 2] = updated
                multipliers[edge // 2] = multipliers_in[at, :] + step_size * direction[at, :]
        else:
            residual[at, :] = updated
            multipliers[at, :] = step_size * direction[at, :]
    block.place()
    block.multiply()
    partial = jnp.zeros((1, cases), jnp.float32)
    current = kept if last else residual
    for edge in range(4):
        out[edge][...] = block.back(edge)
        partial += sum_rows(current[pl.ds(edge * width, width), :] * out[edge][...])
    copies[...] = jnp.broadcast_to(0.5 * partial, copies.shape)


def add_kernel(pieces, copies):
    copies[...] = jnp.broadcast_to(sum(pieces[device] for device in range(pieces.shape[0])), copies.shape)


def finish_kernel(east, north, from_east, from_north, old_direction, pieces, old_aligned, direction):
    width = east.shape[0]
    ratio = sum(pieces[device, 0:1, :] for device in range(pieces.shape[0])) / old_aligned[0:1, :]
    for at, own, received, old in ((0, east, from_east, width), (1, north, from_north, 3 * width)):
        direction[at] = 0.5 * (own[...] - received[...]) + ratio * old_direction[pl.ds(old, width), :]


def piece_cross_labels(corner_map):
    columns, rows, corners = corner_map.shape
    fields = corners // 4

    def corner(at, rows_of):
        return corner_map[:, rows_of, at * fields : (at + 1) * fields]

    sides = [
        jnp.concatenate([corner(east, slice(None)), corner(2 + east, slice(rows - 1, rows))], axis=1)
        for east in range(2)
    ]
    strips = jnp.concatenate([side.reshape(columns, -1) for side in sides], axis=1)
    none = jnp.full((columns, SUMS // 2), -1, corner_map.dtype)
    return jnp.concatenate([strips, none], axis=1).reshape(1, -1)


def body(load_jump, flex, precond, couple, edge_map, flags, corner_map, coarse_factor):
    _, width, cases = load_jump.shape[2:]
    count = 4 * width
    order = edge_map[0, 0]
    flex_local = flex[0, 0]
    precond_local = precond[0, 0]
    couple_local = couple[0, 0]
    column_index = lax.axis_index("gx")
    row_index = lax.axis_index("gy")
    columns = lax.axis_size("gx")
    rows = lax.axis_size("gy")
    coarse_count = coarse_factor.shape[0]
    coarse_size = -(-coarse_count // LANES) * LANES
    strip_rows = 4 * (rows + 1) + SUMS // 2

    inside = jnp.stack([column_index < columns - 1, row_index < rows - 1]).astype(jnp.float32)
    live = flags[0, 0].astype(jnp.float32) * inside[:, None]
    mask_rows = max(width // cases, 1)
    held = jnp.pad(live.reshape(2, mask_rows, -1), ((0, 0), (0, 8 - mask_rows), (0, 0)))
    own = jnp.concatenate([live[:, :, None] * load_jump[0, 0], held], axis=1)
    east, north = own[0], own[1]
    west = shift(east, "gx", 1)
    south = shift(north, "gy", 1)

    piece_labels = piece_cross_labels(corner_map)
    around = jnp.concatenate(
        [
            lax.dynamic_slice(
                corner_map,
                (
                    jnp.clip(column_index + dx, 0, columns - 1),
                    jnp.clip(row_index + dy, 0, rows - 1),
                    0,
                ),
                (1, 1, CORNER_ROWS),
            ).reshape(-1, 1)
            for dx, dy in ((0, 0), (-1, 0), (1, 0), (0, -1), (0, 1))
        ]
    )
    spare = coarse_size - coarse_count
    levels = lax.iota(jnp.int32, coarse_size)
    factor = jnp.pad(coarse_factor, ((0, spare), (0, spare))) + jnp.where(
        (levels[:, None] == levels[None, :]) & (levels[:, None] >= coarse_count), 1.0, 0.0
    )
    forward, backward, back = call(
        prepare_kernel,
        (
            shaped(coarse_size, columns * strip_rows),
            shaped(5 * CORNER_ROWS, coarse_size),
            shaped(CORNER_ROWS, count),
        ),
        (factor, piece_labels, around, couple_local, order[None, :]),
        [pltpu.VMEM((coarse_size, coarse_size), jnp.float32)],
        flops=10**10,
    )

    mask = jnp.concatenate(
        [
            west[width : width + mask_rows].reshape(-1),
            live[0],
            south[width : width + mask_rows].reshape(-1),
            live[1],
        ]
    )
    held_order = jnp.where(mask > 0, order, -1)
    row_order = held_order[None, :]
    column_order = held_order[:, None]
    scratch = block_scratch(count, cases)
    block_flops = 8 * count * count * cases
    message = shaped(width + CORNER_ROWS * max(width // cases, 1), cases)
    edge = shaped(width, cases)
    whole = shaped(count, cases)
    row = shaped(8, cases)

    residual, *sides, total = call(
        smooth_kernel,
        (whole, message, message, message, message, row),
        (west, east, south, north, row_order, column_order, back, mask[None, :], precond_local),
        scratch,
        in_hbm=(8,),
        flops=block_flops,
    )
    received = exchange(*sides)
    multipliers = aligned = direction = pieces = edge_couple = None
    for iteration in range(ITERS):
        first = iteration == 0
        last = iteration == ITERS - 1
        beside = (total,) if first else (direction, pieces, aligned)
        operands = (*sides, *received, *beside, row_order, column_order, couple_local, flex_local)
        direction, *sides, copies, other = call(
            functools.partial(apply_kernel, first),
            (
                whole, edge, edge, edge, edge,
                shaped(rows, CORNER_ROWS + SUMS, cases),
                shaped(2 * CORNER_ROWS, count) if first else row,
            ),
            operands,
            scratch,
            in_hbm=(len(operands) - 1,),
            flops=block_flops,
        )
        if first:
            edge_couple = other
        else:
            aligned = other
        received = exchange(*sides)
        strips = call(strip_kernel, shaped(columns, strip_rows, cases), (swap(copies, "gy"),))
        pieces = swap(strips, "gx")
        operands = (pieces, forward, backward, edge_couple, direction, residual, *sides, *received)
        if not first:
            operands += (multipliers, aligned)
        operands += (row_order, column_order, precond_local)
        kept = shaped(2, width, cases) if last else whole
        residual, multipliers, *sides = call(
            functools.partial(update_kernel, first, last),
            (kept, kept, edge, edge, edge, edge, shaped(rows, 8, cases)) + ((row,) if first else ()),
            operands,
            [pltpu.VMEM((count, cases), jnp.float32) if last else pltpu.VMEM((8, LANES), jnp.float32)]
            + scratch,
            in_hbm=(len(operands) - 1,),
            flops=block_flops,
        )
        if first:
            *sides, copies, aligned = sides
        else:
            *sides, copies = sides
        if last:
            from_east = shift(sides[0], "gx", -1)
            from_north = shift(sides[2], "gy", -1)
        else:
            received = exchange(*sides)
        pieces = swap(call(add_kernel, shaped(columns, 8, cases), (swap(copies, "gy"),)), "gx")
    direction = call(
        finish_kernel,
        shaped(2, width, cases),
        (sides[1], sides[3], from_east, from_north, direction, pieces, aligned),
    )
    return multipliers[None, None], residual[None, None], direction[None, None]


def solution(mesh):
    return jax.shard_map(
        body,
        mesh=mesh,
        in_specs=(
            P("gx", "gy", None, None, None),
            P("gx", "gy", None, None),
            P("gx", "gy", None, None),
            P("gx", "gy", None, None),
            P("gx", "gy", None),
            P("gx", "gy", None, None),
            P(),
            P(),
        ),
        out_specs=(
            P("gx", "gy", None, None, None),
            P("gx", "gy", None, None, None),
            P("gx", "gy", None, None, None),
        ),
        check_vma=False,
    )
```

```python
import functools

import jax
import jax.numpy as jnp
from jax import lax
from jax.experimental import pallas as pl
from jax.experimental.pallas import tpu as pltpu
from jax.sharding import PartitionSpec as P

ITERS = 2
HIGHEST = lax.Precision.HIGHEST
LANES = 128
CORNER_ROWS = 8
SUMS = 8


def shift(shard, axis, by):
    devices = lax.axis_size(axis)
    pairs = [(i, i + by) for i in range(devices) if 0 <= i + by < devices]
    return lax.ppermute(shard, axis, pairs)


def exchange(west, east, south, north):
    return shift(east, "gx", 1), shift(west, "gx", -1), shift(north, "gy", 1), shift(south, "gy", -1)


def gather(piece, axis):
    return lax.all_gather(piece, axis)


def call(kernel, out_shape, operands, scratch_shapes=(), in_hbm=(), flops=0, limit=32):
    vmem = pl.BlockSpec(memory_space=pltpu.VMEM)
    specs = [
        pl.BlockSpec(memory_space=pltpu.HBM) if at in in_hbm else vmem for at in range(len(operands))
    ]
    moved = sum(a.size * a.dtype.itemsize for a in operands)
    return pl.pallas_call(
        kernel,
        out_shape=out_shape,
        in_specs=specs,
        out_specs=jax.tree.map(lambda _: vmem, out_shape),
        scratch_shapes=list(scratch_shapes),
        compiler_params=pltpu.CompilerParams(vmem_limit_bytes=limit * 2**20),
        cost_estimate=pl.CostEstimate(flops=flops, bytes_accessed=moved, transcendentals=0),
    )(*operands)


def shaped(*shape, dtype=jnp.float32):
    return jax.ShapeDtypeStruct(shape, dtype)


def sum_rows(values):
    return jnp.sum(values, axis=0, keepdims=True)


def block_scratch(count, cases):
    tile = min(512, count)
    return [
        pltpu.VMEM((count, count), jnp.bfloat16),
        pltpu.VMEM((count, cases), jnp.bfloat16),
        pltpu.VMEM((count, cases), jnp.bfloat16),
        pltpu.VMEM((count, 2 * cases), jnp.bfloat16),
        pltpu.SemaphoreType.DMA((count // tile,)),
    ]


class Block:
    def __init__(self, matrix_hbm, row_order, column_order, scratch):
        self.matrix_hbm = matrix_hbm
        self.row_order = row_order
        self.column_order = column_order
        self.matrix, self.spread, self.placed, self.parts, self.sems = scratch
        self.count, self.cases = self.spread.shape
        self.tile = min(512, self.count)
        self.tiles = self.count // self.tile

    def rows(self, t):
        return pl.ds(pl.multiple_of(t * self.tile, self.tile), self.tile)

    def fetch(self, t):
        rows = self.rows(t)
        return pltpu.make_async_copy(self.matrix_hbm.at[rows], self.matrix.at[rows], self.sems.at[t])

    def start(self):
        @pl.loop(0, self.tiles)
        def _(t):
            self.fetch(t).start()

    def place(self):
        @pl.loop(0, self.tiles)
        def _(t):
            level = lax.broadcasted_iota(jnp.int32, (self.tile, self.count), 0) + t * self.tile
            select = (level == self.row_order[...]).astype(jnp.bfloat16)
            self.placed[self.rows(t), :] = jnp.dot(
                select, self.spread[...], preferred_element_type=jnp.float32
            ).astype(jnp.bfloat16)

    def multiply(self):
        @pl.loop(0, self.tiles)
        def _(t):
            self.fetch(t).wait()
            product = jnp.dot(
                self.matrix[self.rows(t), :], self.placed[...], preferred_element_type=jnp.float32
            )
            high = product.astype(jnp.bfloat16)
            self.parts[self.rows(t), : self.cases] = high
            self.parts[self.rows(t), self.cases :] = (product - high.astype(jnp.float32)).astype(jnp.bfloat16)

    def back(self, edge):
        level = lax.broadcasted_iota(jnp.int32, (self.count // 4, self.count), 1)
        order = self.column_order[pl.ds(edge * (self.count // 4), self.count // 4), :]
        select = (level == order).astype(jnp.bfloat16)
        both = jnp.dot(select, self.parts[...], preferred_element_type=jnp.float32)
        return both[:, : self.cases] + both[:, self.cases :]


def invert(factor, inverse):
    size = factor.shape[0]
    row = lax.broadcasted_iota(jnp.int32, (LANES, LANES), 0)
    column = lax.broadcasted_iota(jnp.int32, (LANES, LANES), 1)
    blocks = [pl.ds(at, LANES) for at in range(0, size, LANES)]

    def times(left, right):
        return jnp.dot(left, right, precision=HIGHEST, preferred_element_type=jnp.float32)

    inverse[...] = jnp.zeros((size, size), jnp.float32)
    corners = [factor[at, at] for at in blocks]
    solved = [jnp.where(row == column, 1.0 / corner, 0.0) for corner in corners]
    width = 1
    while width < LANES:
        joins = (row // (2 * width) == column // (2 * width)) & (row // width > column // width)
        half = [times(jnp.where(joins, c, 0.0), s) for c, s in zip(corners, solved)]
        solved = [s - times(s, h) for s, h in zip(solved, half)]
        width *= 2
    for n, at in enumerate(blocks):
        if n:
            before = pl.ds(0, n * LANES)
            inverse[at, before] = -times(solved[n], times(factor[at, before], inverse[before, before]))
        inverse[at, at] = solved[n]


def prepare_kernel(factor, piece_labels, corner_labels, couple, row_order, forward, backward, back, inverse):
    invert(factor, inverse)
    size, pieces = forward.shape
    level = lax.broadcasted_iota(jnp.int32, (size, pieces), 0)
    select = (level == piece_labels[...]).astype(jnp.float32)
    forward[...] = jnp.dot(inverse[...], select, precision=HIGHEST, preferred_element_type=jnp.float32)
    level = lax.broadcasted_iota(jnp.int32, backward.shape, 1)
    select = (level == corner_labels[...]).astype(jnp.float32)
    backward[...] = lax.dot_general(
        select, inverse[...], (((1,), (1,)), ((), ())), precision=HIGHEST, preferred_element_type=jnp.float32
    )
    count = couple.shape[1]
    tile = min(512, count)

    @pl.loop(0, count // tile)
    def _(t):
        at = pl.ds(pl.multiple_of(t * tile, tile), tile)
        level = lax.broadcasted_iota(jnp.int32, (count, tile), 0)
        select = (level == row_order[:, at]).astype(jnp.bfloat16)
        back[:, at] = jnp.dot(couple[...], select, preferred_element_type=jnp.float32)


def write_messages(block, messages, back, mask):
    width = block.count // 4
    cut = width // block.cases if width >= block.cases else 1
    for edge, message in enumerate(messages):
        message[pl.ds(0, width), :] = block.back(edge)
        for part in range(cut):
            at = pl.ds(edge * width + part * block.cases, min(block.cases, width))
            message[pl.ds(width + part * CORNER_ROWS, CORNER_ROWS), :] = back[:, at] * mask[:, at]


def smooth_kernel(
    west, east, south, north, row_order, column_order, back, mask, matrix_hbm,
    residual, west_out, east_out, south_out, north_out, total, *scratch,
):
    block = Block(matrix_hbm, row_order, column_order, scratch)
    block.start()
    width = block.count // 4
    for edge, (source, sign) in enumerate(((west, -1.0), (east, 1.0), (south, -1.0), (north, 1.0))):
        at = pl.ds(edge * width, width)
        residual[at, :] = sign * source[pl.ds(0, width), :]
        block.spread[at, :] = (0.5 * residual[at, :]).astype(jnp.bfloat16)
    block.place()
    block.multiply()
    messages = (west_out, east_out, south_out, north_out)
    write_messages(block, messages, back, mask)
    partial = sum(
        sum_rows(residual[pl.ds(edge * width, width), :] * message[pl.ds(0, width), :])
        for edge, message in enumerate(messages)
    )
    total[...] = jnp.broadcast_to(0.5 * partial, total.shape)


def apply_kernel(first, *refs):
    own, refs = refs[:4], refs[4:]
    received, refs = refs[:4], refs[4:]
    if first:
        (total,), refs = refs[:1], refs[1:]
    else:
        (old_direction, pieces, old_aligned), refs = refs[:3], refs[3:]
    row_order, column_order, couple, matrix_hbm = refs[:4]
    direction, refs = refs[4], refs[5:]
    out, refs = refs[:4], refs[4:]
    piece, other = refs[:2]
    block = Block(matrix_hbm, row_order, column_order, refs[2:])
    block.start()
    count, cases = block.count, block.cases
    width = count // 4
    if not first:
        aligned = sum(pieces[device, 0:1, :] for device in range(pieces.shape[0]))
        ratio = aligned / old_aligned[0:1, :]
        other[...] = jnp.broadcast_to(aligned, other.shape)
    for edge in range(4):
        at = pl.ds(edge * width, width)
        smoothed = 0.5 * (own[edge][pl.ds(0, width), :] - received[edge][pl.ds(0, width), :])
        if not first:
            smoothed = smoothed + ratio * old_direction[at, :]
        direction[at, :] = smoothed
        block.spread[at, :] = smoothed.astype(jnp.bfloat16)
    block.place()
    block.multiply()
    curvature = jnp.zeros((1, cases), jnp.float32)
    for edge in range(4):
        at = pl.ds(edge * width, width)
        out[edge][...] = block.back(edge)
        curvature += sum_rows(block.spread[at, :].astype(jnp.float32) * out[edge][...])
    terms = jnp.dot(couple[...], block.placed[...], preferred_element_type=jnp.float32)
    row = lax.broadcasted_iota(jnp.int32, (SUMS, cases), 0)
    sums = jnp.where(row == 0, curvature, 0.0)
    if first:
        sums = sums + jnp.where(row == 1, total[0:1, :], 0.0)
        cut = max(width // cases, 1)
        span = min(width, cases)
        for edge in range(4):
            for part in range(cut):
                at = pl.ds(edge * width + part * span, span)
                rows = pl.ds(width + part * CORNER_ROWS, CORNER_ROWS)
                other[pl.ds(0, CORNER_ROWS), at] = own[edge][rows, :]
                other[pl.ds(CORNER_ROWS, CORNER_ROWS), at] = -received[edge][rows, :]
    piece[pl.ds(0, CORNER_ROWS), :] = terms
    piece[pl.ds(CORNER_ROWS, SUMS), :] = sums


def strip_kernel(pieces, strip):
    devices, piece, cases = pieces.shape
    rows = strip.shape[0]
    half = 2 * (devices + 1)
    row = lax.broadcasted_iota(jnp.int32, (rows, devices * piece), 0)
    source = lax.broadcasted_iota(jnp.int32, (rows, devices * piece), 1)
    device, term = source // piece, source % piece
    target = (term // 2) % 2 * half + (device + term // 4) * 2 + term % 2
    target = jnp.where(term < CORNER_ROWS, target, 2 * half + term - CORNER_ROWS)
    select = (row == target).astype(jnp.float32)
    strip[...] = jnp.dot(
        select,
        pieces[...].reshape(devices * piece, cases),
        precision=HIGHEST,
        preferred_element_type=jnp.float32,
    )


def update_kernel(first, last, *refs):
    pieces, forward, backward, edge_couple, direction, residual_in = refs[:6]
    own, refs = refs[6:10], refs[10:]
    received, refs = refs[:4], refs[4:]
    if not first:
        (multipliers_in, old_aligned), refs = refs[:2], refs[2:]
    row_order, column_order, matrix_hbm = refs[:3]
    residual, multipliers = refs[3:5]
    out, refs = refs[5:9], refs[9:]
    total = refs[0]
    if first:
        aligned_out, refs = refs[1], refs[2:]
    else:
        refs = refs[1:]
    kept, *scratch = refs
    block = Block(matrix_hbm, row_order, column_order, scratch)
    block.start()
    count, cases = block.count, block.cases
    width = count // 4
    devices, piece, _ = pieces.shape
    scalar_row = piece - SUMS // 2
    sums = sum(pieces[device, pl.ds(scalar_row, SUMS // 2), :] for device in range(devices))
    half_solved = jnp.dot(
        forward[...],
        pieces[...].reshape(devices * piece, cases),
        precision=HIGHEST,
        preferred_element_type=jnp.float32,
    )
    corners = jnp.dot(backward[...], half_solved, precision=HIGHEST, preferred_element_type=jnp.float32)
    curvature = sums[0:1, :] + sum_rows(half_solved * half_solved)
    if first:
        aligned = sums[1:2, :]
        aligned_out[...] = jnp.broadcast_to(aligned, aligned_out.shape)
    else:
        aligned = old_aligned[0:1, :]
    step_size = aligned / curvature
    for edge in range(4):
        at = pl.ds(edge * width, width)
        beyond = pl.ds((edge + 1) * CORNER_ROWS, CORNER_ROWS)
        solved = jnp.concatenate(
            [corners[0:CORNER_ROWS], corners[(edge + 1) * CORNER_ROWS : (edge + 2) * CORNER_ROWS]]
        )
        high = solved.astype(jnp.bfloat16)
        rest = solved - high.astype(jnp.float32)
        middle = rest.astype(jnp.bfloat16)
        low = (rest - middle.astype(jnp.float32)).astype(jnp.bfloat16)
        coupling = edge_couple[:, at].astype(jnp.bfloat16)
        coarse = lax.dot_general(
            jnp.concatenate([coupling] * 3),
            jnp.concatenate([high, middle, low]),
            (((0,), (0,)), ((), ())),
            preferred_element_type=jnp.float32,
        )
        image = own[edge][...] - received[edge][...] + coarse
        updated = residual_in[at, :] - step_size * image
        block.spread[at, :] = (0.5 * updated).astype(jnp.bfloat16)
        if last:
            kept[at, :] = updated
            if edge % 2:
                residual[edge // 2] = updated
                multipliers[edge // 2] = multipliers_in[at, :] + step_size * direction[at, :]
        else:
            residual[at, :] = updated
            multipliers[at, :] = step_size * direction[at, :]
    block.place()
    block.multiply()
    partial = jnp.zeros((1, cases), jnp.float32)
    current = kept if last else residual
    for edge in range(4):
        out[edge][...] = block.back(edge)
        partial += sum_rows(current[pl.ds(edge * width, width), :] * out[edge][...])
    total[...] = jnp.broadcast_to(0.5 * partial, total.shape)


def add_kernel(pieces, total):
    total[...] = sum(pieces[device] for device in range(pieces.shape[0]))


def finish_kernel(east, north, from_east, from_north, old_direction, pieces, old_aligned, direction):
    width = east.shape[0]
    ratio = sum(pieces[device, 0:1, :] for device in range(pieces.shape[0])) / old_aligned[0:1, :]
    for at, own, received, old in ((0, east, from_east, width), (1, north, from_north, 3 * width)):
        direction[at] = 0.5 * (own[...] - received[...]) + ratio * old_direction[pl.ds(old, width), :]


def piece_cross_labels(corner_map):
    columns, rows, corners = corner_map.shape
    fields = corners // 4

    def corner(at, rows_of):
        return corner_map[:, rows_of, at * fields : (at + 1) * fields]

    sides = [
        jnp.concatenate([corner(east, slice(None)), corner(2 + east, slice(rows - 1, rows))], axis=1)
        for east in range(2)
    ]
    strips = jnp.concatenate([side.reshape(columns, -1) for side in sides], axis=1)
    none = jnp.full((columns, SUMS // 2), -1, corner_map.dtype)
    return jnp.concatenate([strips, none], axis=1).reshape(1, -1)


def body(load_jump, flex, precond, couple, edge_map, flags, corner_map, coarse_factor):
    _, width, cases = load_jump.shape[2:]
    count = 4 * width
    order = edge_map[0, 0]
    flex_local = flex[0, 0]
    precond_local = precond[0, 0]
    couple_local = couple[0, 0]
    column_index = lax.axis_index("gx")
    row_index = lax.axis_index("gy")
    columns = lax.axis_size("gx")
    rows = lax.axis_size("gy")
    coarse_count = coarse_factor.shape[0]
    coarse_size = -(-coarse_count // LANES) * LANES
    strip_rows = 4 * (rows + 1) + SUMS // 2

    inside = jnp.stack([column_index < columns - 1, row_index < rows - 1]).astype(jnp.float32)
    live = flags[0, 0].astype(jnp.float32) * inside[:, None]
    mask_rows = max(width // cases, 1)
    held = jnp.pad(live.reshape(2, mask_rows, -1), ((0, 0), (0, 8 - mask_rows), (0, 0)))
    own = jnp.concatenate([live[:, :, None] * load_jump[0, 0], held], axis=1)
    east, north = own[0], own[1]
    west = shift(east, "gx", 1)
    south = shift(north, "gy", 1)

    piece_labels = piece_cross_labels(corner_map)
    around = jnp.concatenate(
        [
            lax.dynamic_slice(
                corner_map,
                (
                    jnp.clip(column_index + dx, 0, columns - 1),
                    jnp.clip(row_index + dy, 0, rows - 1),
                    0,
                ),
                (1, 1, CORNER_ROWS),
            ).reshape(-1, 1)
            for dx, dy in ((0, 0), (-1, 0), (1, 0), (0, -1), (0, 1))
        ]
    )
    spare = coarse_size - coarse_count
    levels = lax.iota(jnp.int32, coarse_size)
    factor = jnp.pad(coarse_factor, ((0, spare), (0, spare))) + jnp.where(
        (levels[:, None] == levels[None, :]) & (levels[:, None] >= coarse_count), 1.0, 0.0
    )
    forward, backward, back = call(
        prepare_kernel,
        (
            shaped(coarse_size, columns * strip_rows),
            shaped(5 * CORNER_ROWS, coarse_size),
            shaped(CORNER_ROWS, count),
        ),
        (factor, piece_labels, around, couple_local, order[None, :]),
        [pltpu.VMEM((coarse_size, coarse_size), jnp.float32)],
        flops=10**10,
    )

    mask = jnp.concatenate(
        [
            west[width : width + mask_rows].reshape(-1),
            live[0],
            south[width : width + mask_rows].reshape(-1),
            live[1],
        ]
    )
    held_order = jnp.where(mask > 0, order, -1)
    row_order = held_order[None, :]
    column_order = held_order[:, None]
    scratch = block_scratch(count, cases)
    block_flops = 8 * count * count * cases
    message = shaped(width + CORNER_ROWS * max(width // cases, 1), cases)
    edge = shaped(width, cases)
    whole = shaped(count, cases)
    row = shaped(8, cases)

    residual, *sides, total = call(
        smooth_kernel,
        (whole, message, message, message, message, row),
        (west, east, south, north, row_order, column_order, back, mask[None, :], precond_local),
        scratch,
        in_hbm=(8,),
        flops=block_flops,
    )
    received = exchange(*sides)
    multipliers = aligned = direction = pieces = edge_couple = None
    for iteration in range(ITERS):
        first = iteration == 0
        last = iteration == ITERS - 1
        beside = (total,) if first else (direction, pieces, aligned)
        operands = (*sides, *received, *beside, row_order, column_order, couple_local, flex_local)
        direction, *sides, piece, other = call(
            functools.partial(apply_kernel, first),
            (
                whole, edge, edge, edge, edge,
                shaped(CORNER_ROWS + SUMS, cases),
                shaped(2 * CORNER_ROWS, count) if first else row,
            ),
            operands,
            scratch,
            in_hbm=(len(operands) - 1,),
            flops=block_flops,
        )
        if first:
            edge_couple = other
        else:
            aligned = other
        received = exchange(*sides)
        strip = call(strip_kernel, shaped(strip_rows, cases), (gather(piece, "gy"),))
        pieces = gather(strip, "gx")
        operands = (pieces, forward, backward, edge_couple, direction, residual, *sides, *received)
        if not first:
            operands += (multipliers, aligned)
        operands += (row_order, column_order, precond_local)
        kept = shaped(2, width, cases) if last else whole
        residual, multipliers, *sides = call(
            functools.partial(update_kernel, first, last),
            (kept, kept, edge, edge, edge, edge, row) + ((row,) if first else ()),
            operands,
            [pltpu.VMEM((count, cases), jnp.float32) if last else pltpu.VMEM((8, LANES), jnp.float32)]
            + scratch,
            in_hbm=(len(operands) - 1,),
            flops=block_flops,
        )
        if first:
            *sides, total, aligned = sides
        else:
            *sides, total = sides
        if last:
            from_east = shift(sides[0], "gx", -1)
            from_north = shift(sides[2], "gy", -1)
        else:
            received = exchange(*sides)
        pieces = gather(call(add_kernel, row, (gather(total, "gy"),)), "gx")
    direction = call(
        finish_kernel,
        shaped(2, width, cases),
        (sides[1], sides[3], from_east, from_north, direction, pieces, aligned),
    )
    return multipliers[None, None], residual[None, None], direction[None, None]


def solution(mesh):
    return jax.shard_map(
        body,
        mesh=mesh,
        in_specs=(
            P("gx", "gy", None, None, None),
            P("gx", "gy", None, None),
            P("gx", "gy", None, None),
            P("gx", "gy", None, None),
            P("gx", "gy", None),
            P("gx", "gy", None, None),
            P(),
            P(),
        ),
        out_specs=(
            P("gx", "gy", None, None, None),
            P("gx", "gy", None, None, None),
            P("gx", "gy", None, None, None),
        ),
        check_vma=False,
    )
```

```python
import functools

import jax
import jax.numpy as jnp
from jax import lax
from jax.experimental import pallas as pl
from jax.experimental.pallas import tpu as pltpu
from jax.sharding import PartitionSpec as P

ITERS = 2
HIGHEST = lax.Precision.HIGHEST
LANES = 128
CORNER_ROWS = 8
SUMS = 8


def shift(shard, axis, by):
    devices = lax.axis_size(axis)
    pairs = [(i, i + by) for i in range(devices) if 0 <= i + by < devices]
    return lax.ppermute(shard, axis, pairs)


def exchange(west, east, south, north):
    return shift(east, "gx", 1), shift(west, "gx", -1), shift(north, "gy", 1), shift(south, "gy", -1)


def swap(copies, axis):
    return lax.all_to_all(copies, axis, 0, 0, tiled=True)


def call(kernel, out_shape, operands, scratch_shapes=(), in_hbm=(), flops=0, limit=46):
    vmem = pl.BlockSpec(memory_space=pltpu.VMEM)
    specs = [
        pl.BlockSpec(memory_space=pl.ANY) if at in in_hbm else vmem for at in range(len(operands))
    ]
    moved = sum(a.size * a.dtype.itemsize for a in operands)
    return pl.pallas_call(
        kernel,
        out_shape=out_shape,
        in_specs=specs,
        out_specs=jax.tree.map(lambda _: vmem, out_shape),
        scratch_shapes=list(scratch_shapes),
        compiler_params=pltpu.CompilerParams(vmem_limit_bytes=limit * 2**20),
        cost_estimate=pl.CostEstimate(flops=flops, bytes_accessed=moved, transcendentals=0),
    )(*operands)


def shaped(*shape, dtype=jnp.float32):
    return jax.ShapeDtypeStruct(shape, dtype)


def sum_rows(values):
    return jnp.sum(values, axis=0, keepdims=True)


def over_cases(row, cases):
    first = lax.broadcasted_iota(jnp.int32, (16, row.shape[1]), 0) == 0
    rows = jnp.where(first, jnp.broadcast_to(row, first.shape), 0.0).astype(jnp.bfloat16)
    ones = jnp.ones((16, cases), jnp.bfloat16)
    return lax.dot_general(rows, ones, (((0,), (0,)), ((), ())), preferred_element_type=jnp.float32)


def block_scratch(count, cases):
    tile = min(512, count)
    return [
        pltpu.VMEM((count, count), jnp.bfloat16),
        pltpu.VMEM((count, cases), jnp.bfloat16),
        pltpu.VMEM((count, cases), jnp.bfloat16),
        pltpu.VMEM((count, 2 * cases), jnp.bfloat16),
        pltpu.SemaphoreType.DMA((count // tile,)),
    ]


class Block:
    def __init__(self, matrix_hbm, row_order, column_order, scratch):
        self.matrix_hbm = matrix_hbm
        self.row_order = row_order
        self.column_order = column_order
        self.matrix, self.spread, self.placed, self.parts, self.sems = scratch
        self.count, self.cases = self.spread.shape
        self.tile = min(512, self.count)
        self.tiles = self.count // self.tile

    def rows(self, t):
        return pl.ds(pl.multiple_of(t * self.tile, self.tile), self.tile)

    def fetch(self, t):
        rows = self.rows(t)
        return pltpu.make_async_copy(self.matrix_hbm.at[rows], self.matrix.at[rows], self.sems.at[t])

    def start(self):
        @pl.loop(0, self.tiles)
        def _(t):
            self.fetch(t).start()

    def place(self):
        @pl.loop(0, self.tiles)
        def _(t):
            level = lax.broadcasted_iota(jnp.int32, (self.tile, self.count), 0) + t * self.tile
            select = (level == self.row_order[...]).astype(jnp.bfloat16)
            self.placed[self.rows(t), :] = jnp.dot(
                select, self.spread[...], preferred_element_type=jnp.float32
            ).astype(jnp.bfloat16)

    def multiply(self):
        @pl.loop(0, self.tiles)
        def _(t):
            self.fetch(t).wait()
            product = jnp.dot(
                self.matrix[self.rows(t), :], self.placed[...], preferred_element_type=jnp.float32
            )
            high = product.astype(jnp.bfloat16)
            self.parts[self.rows(t), : self.cases] = high
            self.parts[self.rows(t), self.cases :] = (product - high.astype(jnp.float32)).astype(jnp.bfloat16)

    def back(self, edge, mask):
        level = lax.broadcasted_iota(jnp.int32, (self.count // 4, self.count), 1)
        order = self.column_order[pl.ds(edge * (self.count // 4), self.count // 4), :]
        select = (level == order).astype(jnp.bfloat16)
        both = jnp.dot(select, self.parts[...], preferred_element_type=jnp.float32)
        held = over_cases(mask[pl.ds(edge, 1), :], self.cases)
        return (both[:, : self.cases] + both[:, self.cases :]) * held


def invert(factor, inverse):
    size = factor.shape[0]
    row = lax.broadcasted_iota(jnp.int32, (LANES, LANES), 0)
    column = lax.broadcasted_iota(jnp.int32, (LANES, LANES), 1)
    blocks = [pl.ds(at, LANES) for at in range(0, size, LANES)]

    def times(left, right):
        return jnp.dot(left, right, precision=HIGHEST, preferred_element_type=jnp.float32)

    inverse[...] = jnp.zeros((size, size), jnp.float32)
    corners = [factor[at, at] for at in blocks]
    solved = [jnp.where(row == column, 1.0 / corner, 0.0) for corner in corners]
    width = 1
    while width < LANES:
        joins = (row // (2 * width) == column // (2 * width)) & (row // width > column // width)
        half = [times(jnp.where(joins, c, 0.0), s) for c, s in zip(corners, solved)]
        solved = [s - times(s, h) for s, h in zip(solved, half)]
        width *= 2
    for n, at in enumerate(blocks):
        if n:
            before = pl.ds(0, n * LANES)
            inverse[at, before] = -times(solved[n], times(factor[at, before], inverse[before, before]))
        inverse[at, at] = solved[n]


def prepare_kernel(factor, piece_labels, corner_labels, couple, row_order, forward, backward, back, inverse):
    invert(factor, inverse)
    size, pieces = forward.shape
    level = lax.broadcasted_iota(jnp.int32, (size, pieces), 0)
    select = (level == piece_labels[...]).astype(jnp.float32)
    forward[...] = jnp.dot(inverse[...], select, precision=HIGHEST, preferred_element_type=jnp.float32)
    level = lax.broadcasted_iota(jnp.int32, backward.shape, 1)
    select = (level == corner_labels[...]).astype(jnp.float32)
    backward[...] = lax.dot_general(
        select, inverse[...], (((1,), (1,)), ((), ())), precision=HIGHEST, preferred_element_type=jnp.float32
    )
    count = couple.shape[1]
    tile = min(512, count)

    @pl.loop(0, count // tile)
    def _(t):
        at = pl.ds(pl.multiple_of(t * tile, tile), tile)
        level = lax.broadcasted_iota(jnp.int32, (count, tile), 0)
        select = (level == row_order[:, at]).astype(jnp.bfloat16)
        back[:, at] = jnp.dot(couple[...], select, preferred_element_type=jnp.float32)


def smooth_kernel(
    west, east, south, north, row_order, column_order, back, matrix_hbm,
    residual, west_out, east_out, south_out, north_out, total, mask, *scratch,
):
    block = Block(matrix_hbm, row_order, column_order, scratch)
    block.start()
    width, cases = block.count // 4, block.cases
    span = min(cases, width)
    messages = (west_out, east_out, south_out, north_out)
    for edge, (source, sign) in enumerate(((west, -1.0), (east, 1.0), (south, -1.0), (north, 1.0))):
        at = pl.ds(edge * width, width)
        residual[at, :] = sign * source[pl.ds(0, width), :]
        block.spread[at, :] = (0.5 * residual[at, :]).astype(jnp.bfloat16)
        for part in range(width // span):
            held = source[pl.ds(width + part, 1), :]
            mask[pl.ds(edge, 1), pl.ds(part * span, span)] = held
            messages[edge][pl.ds(width + part * CORNER_ROWS, CORNER_ROWS), :] = (
                back[:, pl.ds(edge * width + part * span, span)] * held
            )
    block.place()
    block.multiply()
    partial = jnp.zeros((1, cases), jnp.float32)
    for edge, message in enumerate(messages):
        sides = block.back(edge, mask)
        message[pl.ds(0, width), :] = sides
        partial += sum_rows(residual[pl.ds(edge * width, width), :] * sides)
    total[...] = jnp.broadcast_to(0.5 * partial, total.shape)


def apply_kernel(first, *refs):
    own, refs = refs[:4], refs[4:]
    received, refs = refs[:4], refs[4:]
    if first:
        (total,), refs = refs[:1], refs[1:]
    else:
        (old_direction, pieces, old_aligned), refs = refs[:3], refs[3:]
    row_order, column_order, mask, couple, matrix_hbm = refs[:5]
    direction, refs = refs[5], refs[6:]
    out, refs = refs[:4], refs[4:]
    copies, other = refs[:2]
    block = Block(matrix_hbm, row_order, column_order, refs[2:])
    block.start()
    count, cases = block.count, block.cases
    width = count // 4
    if not first:
        aligned = sum(pieces[device, 0:1, :] for device in range(pieces.shape[0]))
        ratio = aligned / old_aligned[0:1, :]
        other[...] = jnp.broadcast_to(aligned, other.shape)
    for edge in range(4):
        at = pl.ds(edge * width, width)
        smoothed = 0.5 * (own[edge][pl.ds(0, width), :] - received[edge][pl.ds(0, width), :])
        if not first:
            smoothed = smoothed + ratio * old_direction[at, :]
        direction[at, :] = smoothed
        block.spread[at, :] = smoothed.astype(jnp.bfloat16)
    block.place()
    block.multiply()
    curvature = jnp.zeros((1, cases), jnp.float32)
    for edge in range(4):
        at = pl.ds(edge * width, width)
        out[edge][...] = block.back(edge, mask)
        curvature += sum_rows(block.spread[at, :].astype(jnp.float32) * out[edge][...])
    terms = jnp.dot(couple[...], block.placed[...], preferred_element_type=jnp.float32)
    row = lax.broadcasted_iota(jnp.int32, (SUMS, cases), 0)
    sums = jnp.where(row == 0, curvature, 0.0)
    if first:
        sums = sums + jnp.where(row == 1, total[0:1, :], 0.0)
        cut = max(width // cases, 1)
        span = min(width, cases)
        for edge in range(4):
            for part in range(cut):
                at = pl.ds(edge * width + part * span, span)
                rows = pl.ds(width + part * CORNER_ROWS, CORNER_ROWS)
                other[pl.ds(0, CORNER_ROWS), at] = own[edge][rows, :]
                other[pl.ds(CORNER_ROWS, CORNER_ROWS), at] = -received[edge][rows, :]
    for device in range(copies.shape[0]):
        copies[device, pl.ds(0, CORNER_ROWS), :] = terms
        copies[device, pl.ds(CORNER_ROWS, SUMS), :] = sums


def strip_kernel(pieces, copies):
    devices, piece, cases = pieces.shape
    rows = copies.shape[1]
    half = 2 * (devices + 1)
    row = lax.broadcasted_iota(jnp.int32, (rows, devices * piece), 0)
    source = lax.broadcasted_iota(jnp.int32, (rows, devices * piece), 1)
    device, term = source // piece, source % piece
    target = (term // 2) % 2 * half + (device + term // 4) * 2 + term % 2
    target = jnp.where(term < CORNER_ROWS, target, 2 * half + term - CORNER_ROWS)
    select = (row == target).astype(jnp.float32)
    strip = jnp.dot(
        select,
        pieces[...].reshape(devices * piece, cases),
        precision=HIGHEST,
        preferred_element_type=jnp.float32,
    )
    for device in range(copies.shape[0]):
        copies[device] = strip


def update_kernel(first, last, *refs):
    pieces, forward, backward, edge_couple, direction, residual_in = refs[:6]
    own, refs = refs[6:10], refs[10:]
    received, refs = refs[:4], refs[4:]
    if not first:
        (multipliers_in, old_aligned), refs = refs[:2], refs[2:]
    row_order, column_order, mask, matrix_hbm = refs[:4]
    residual, multipliers = refs[4:6]
    out, refs = refs[6:10], refs[10:]
    copies = refs[0]
    if first:
        aligned_out, refs = refs[1], refs[2:]
    else:
        refs = refs[1:]
    kept, *scratch = refs
    block = Block(matrix_hbm, row_order, column_order, scratch)
    block.start()
    count, cases = block.count, block.cases
    width = count // 4
    devices, piece, _ = pieces.shape
    scalar_row = piece - SUMS // 2
    sums = sum(pieces[device, pl.ds(scalar_row, SUMS // 2), :] for device in range(devices))
    half_solved = jnp.dot(
        forward[...],
        pieces[...].reshape(devices * piece, cases),
        precision=HIGHEST,
        preferred_element_type=jnp.float32,
    )
    corners = jnp.dot(backward[...], half_solved, precision=HIGHEST, preferred_element_type=jnp.float32)
    curvature = sums[0:1, :] + sum_rows(half_solved * half_solved)
    if first:
        aligned = sums[1:2, :]
        aligned_out[...] = jnp.broadcast_to(aligned, aligned_out.shape)
    else:
        aligned = old_aligned[0:1, :]
    step_size = aligned / curvature
    for edge in range(4):
        at = pl.ds(edge * width, width)
        beyond = pl.ds((edge + 1) * CORNER_ROWS, CORNER_ROWS)
        solved = jnp.concatenate(
            [corners[0:CORNER_ROWS], corners[(edge + 1) * CORNER_ROWS : (edge + 2) * CORNER_ROWS]]
        )
        high = solved.astype(jnp.bfloat16)
        rest = solved - high.astype(jnp.float32)
        middle = rest.astype(jnp.bfloat16)
        low = (rest - middle.astype(jnp.float32)).astype(jnp.bfloat16)
        coupling = edge_couple[:, at].astype(jnp.bfloat16)
        coarse = lax.dot_general(
            jnp.concatenate([coupling] * 3),
            jnp.concatenate([high, middle, low]),
            (((0,), (0,)), ((), ())),
            preferred_element_type=jnp.float32,
        )
        image = own[edge][...] - received[edge][...] + coarse
        updated = residual_in[at, :] - step_size * image
        block.spread[at, :] = (0.5 * updated).astype(jnp.bfloat16)
        if last:
            kept[at, :] = updated
            if edge % 2:
                residual[edge // 2] = updated
                multipliers[edge // 2] = multipliers_in[at, :] + step_size * direction[at, :]
        else:
            residual[at, :] = updated
            multipliers[at, :] = step_size * direction[at, :]
    block.place()
    block.multiply()
    partial = jnp.zeros((1, cases), jnp.float32)
    current = kept if last else residual
    for edge in range(4):
        out[edge][...] = block.back(edge, mask)
        partial += sum_rows(current[pl.ds(edge * width, width), :] * out[edge][...])
    copies[...] = jnp.broadcast_to(0.5 * partial, copies.shape)


def add_kernel(pieces, copies):
    copies[...] = jnp.broadcast_to(sum(pieces[device] for device in range(pieces.shape[0])), copies.shape)


def finish_kernel(east, north, from_east, from_north, old_direction, pieces, old_aligned, direction):
    width = east.shape[0]
    ratio = sum(pieces[device, 0:1, :] for device in range(pieces.shape[0])) / old_aligned[0:1, :]
    for at, own, received, old in ((0, east, from_east, width), (1, north, from_north, 3 * width)):
        direction[at] = 0.5 * (own[...] - received[...]) + ratio * old_direction[pl.ds(old, width), :]


def piece_cross_labels(corner_map):
    columns, rows, corners = corner_map.shape
    fields = corners // 4

    def corner(at, rows_of):
        return corner_map[:, rows_of, at * fields : (at + 1) * fields]

    sides = [
        jnp.concatenate([corner(east, slice(None)), corner(2 + east, slice(rows - 1, rows))], axis=1)
        for east in range(2)
    ]
    strips = jnp.concatenate([side.reshape(columns, -1) for side in sides], axis=1)
    none = jnp.full((columns, SUMS // 2), -1, corner_map.dtype)
    return jnp.concatenate([strips, none], axis=1).reshape(1, -1)


def body(load_jump, flex, precond, couple, edge_map, flags, corner_map, coarse_factor):
    _, width, cases = load_jump.shape[2:]
    count = 4 * width
    order = edge_map[0, 0]
    flex_local = flex[0, 0]
    precond_local = precond[0, 0]
    couple_local = couple[0, 0]
    column_index = lax.axis_index("gx")
    row_index = lax.axis_index("gy")
    columns = lax.axis_size("gx")
    rows = lax.axis_size("gy")
    coarse_count = coarse_factor.shape[0]
    coarse_size = -(-coarse_count // LANES) * LANES
    strip_rows = 4 * (rows + 1) + SUMS // 2

    inside = jnp.stack([column_index < columns - 1, row_index < rows - 1]).astype(jnp.float32)
    live = flags[0, 0].astype(jnp.float32) * inside[:, None]
    mask_rows = max(width // cases, 1)
    held = jnp.pad(live.reshape(2, mask_rows, -1), ((0, 0), (0, 8 - mask_rows), (0, 0)))
    own = jnp.concatenate([live[:, :, None] * load_jump[0, 0], held], axis=1)
    east, north = own[0], own[1]
    west = shift(east, "gx", 1)
    south = shift(north, "gy", 1)

    piece_labels = piece_cross_labels(corner_map)
    around = jnp.concatenate(
        [
            lax.dynamic_slice(
                corner_map,
                (
                    jnp.clip(column_index + dx, 0, columns - 1),
                    jnp.clip(row_index + dy, 0, rows - 1),
                    0,
                ),
                (1, 1, CORNER_ROWS),
            ).reshape(-1, 1)
            for dx, dy in ((0, 0), (-1, 0), (1, 0), (0, -1), (0, 1))
        ]
    )
    spare = coarse_size - coarse_count
    levels = lax.iota(jnp.int32, coarse_size)
    factor = jnp.pad(coarse_factor, ((0, spare), (0, spare))) + jnp.where(
        (levels[:, None] == levels[None, :]) & (levels[:, None] >= coarse_count), 1.0, 0.0
    )
    forward, backward, back = call(
        prepare_kernel,
        (
            shaped(coarse_size, columns * strip_rows),
            shaped(5 * CORNER_ROWS, coarse_size),
            shaped(CORNER_ROWS, count),
        ),
        (factor, piece_labels, around, couple_local, order[None, :]),
        [pltpu.VMEM((coarse_size, coarse_size), jnp.float32)],
        flops=10**10,
    )

    row_order = order[None, :]
    column_order = order[:, None]
    scratch = block_scratch(count, cases)
    block_flops = 8 * count * count * cases
    message = shaped(width + CORNER_ROWS * max(width // cases, 1), cases)
    edge = shaped(width, cases)
    whole = shaped(count, cases)
    row = shaped(8, cases)

    residual, *sides, total, mask = call(
        smooth_kernel,
        (whole, message, message, message, message, row, shaped(4, width)),
        (west, east, south, north, row_order, column_order, back, precond_local),
        scratch,
        in_hbm=(7,),
        flops=block_flops,
    )
    received = exchange(*sides)
    multipliers = aligned = direction = pieces = edge_couple = None
    for iteration in range(ITERS):
        first = iteration == 0
        last = iteration == ITERS - 1
        beside = (total,) if first else (direction, pieces, aligned)
        operands = (*sides, *received, *beside, row_order, column_order, mask, couple_local, flex_local)
        direction, *sides, copies, other = call(
            functools.partial(apply_kernel, first),
            (
                whole, edge, edge, edge, edge,
                shaped(rows, CORNER_ROWS + SUMS, cases),
                shaped(2 * CORNER_ROWS, count) if first else row,
            ),
            operands,
            scratch,
            in_hbm=(len(operands) - 1,),
            flops=block_flops,
        )
        if first:
            edge_couple = other
        else:
            aligned = other
        *across, from_south, from_north = exchange(*sides)
        from_south, from_north, copies = lax.optimization_barrier((from_south, from_north, copies))
        received = (*across, from_south, from_north)
        strips = call(strip_kernel, shaped(columns, strip_rows, cases), (swap(copies, "gy"),))
        pieces = swap(strips, "gx")
        operands = (pieces, forward, backward, edge_couple, direction, residual, *sides, *received)
        if not first:
            operands += (multipliers, aligned)
        operands += (row_order, column_order, mask, precond_local)
        kept = shaped(2, width, cases) if last else whole
        residual, multipliers, *sides = call(
            functools.partial(update_kernel, first, last),
            (kept, kept, edge, edge, edge, edge, shaped(rows, 8, cases)) + ((row,) if first else ()),
            operands,
            [pltpu.VMEM((count, cases), jnp.float32) if last else pltpu.VMEM((8, LANES), jnp.float32)]
            + scratch,
            in_hbm=(len(operands) - 1,),
            flops=block_flops,
        )
        if first:
            *sides, copies, aligned = sides
        else:
            *sides, copies = sides
        if last:
            from_east = shift(sides[0], "gx", -1)
            from_north = shift(sides[2], "gy", -1)
        else:
            received = exchange(*sides)
        pieces = swap(call(add_kernel, shaped(columns, 8, cases), (swap(copies, "gy"),)), "gx")
    direction = call(
        finish_kernel,
        shaped(2, width, cases),
        (sides[1], sides[3], from_east, from_north, direction, pieces, aligned),
    )
    return multipliers[None, None], residual[None, None], direction[None, None]


def solution(mesh):
    return jax.shard_map(
        body,
        mesh=mesh,
        in_specs=(
            P("gx", "gy", None, None, None),
            P("gx", "gy", None, None),
            P("gx", "gy", None, None),
            P("gx", "gy", None, None),
            P("gx", "gy", None),
            P("gx", "gy", None, None),
            P(),
            P(),
        ),
        out_specs=(
            P("gx", "gy", None, None, None),
            P("gx", "gy", None, None, None),
            P("gx", "gy", None, None, None),
        ),
        check_vma=False,
    )
```

```python
import functools

import jax
import jax.numpy as jnp
from jax import lax
from jax.experimental import pallas as pl
from jax.experimental.pallas import tpu as pltpu
from jax.sharding import PartitionSpec as P

ITERS = 2
HIGHEST = lax.Precision.HIGHEST
LANES = 128
CORNER_ROWS = 8
SUMS = 8


def shift(shard, axis, by):
    devices = lax.axis_size(axis)
    pairs = [(i, i + by) for i in range(devices) if 0 <= i + by < devices]
    return lax.ppermute(shard, axis, pairs)


def exchange(west, east, south, north):
    return shift(east, "gx", 1), shift(west, "gx", -1), shift(north, "gy", 1), shift(south, "gy", -1)


def swap(copies, axis):
    return lax.all_to_all(copies, axis, 0, 0, tiled=True)


def call(kernel, out_shape, operands, scratch_shapes=(), in_hbm=(), flops=0, limit=46):
    vmem = pl.BlockSpec(memory_space=pltpu.VMEM)
    specs = [
        pl.BlockSpec(memory_space=pl.ANY) if at in in_hbm else vmem for at in range(len(operands))
    ]
    moved = sum(a.size * a.dtype.itemsize for a in operands)
    return pl.pallas_call(
        kernel,
        out_shape=out_shape,
        in_specs=specs,
        out_specs=jax.tree.map(lambda _: vmem, out_shape),
        scratch_shapes=list(scratch_shapes),
        compiler_params=pltpu.CompilerParams(vmem_limit_bytes=limit * 2**20),
        cost_estimate=pl.CostEstimate(flops=flops, bytes_accessed=moved, transcendentals=0),
    )(*operands)


def shaped(*shape, dtype=jnp.float32):
    return jax.ShapeDtypeStruct(shape, dtype)


def sum_rows(values):
    return jnp.sum(values, axis=0, keepdims=True)


def over_cases(row, cases):
    first = lax.broadcasted_iota(jnp.int32, (16, row.shape[1]), 0) == 0
    rows = jnp.where(first, jnp.broadcast_to(row, first.shape), 0.0).astype(jnp.bfloat16)
    ones = jnp.ones((16, cases), jnp.bfloat16)
    return lax.dot_general(rows, ones, (((0,), (0,)), ((), ())), preferred_element_type=jnp.float32)


def block_scratch(count, cases):
    tile = min(512, count)
    return [
        pltpu.VMEM((count, count), jnp.bfloat16),
        pltpu.VMEM((count, cases), jnp.bfloat16),
        pltpu.VMEM((count, cases), jnp.bfloat16),
        pltpu.VMEM((count, 2 * cases), jnp.bfloat16),
        pltpu.SemaphoreType.DMA((count // tile,)),
    ]


class Block:
    def __init__(self, matrix_hbm, row_order, column_order, scratch):
        self.matrix_hbm = matrix_hbm
        self.row_order = row_order
        self.column_order = column_order
        self.matrix, self.spread, self.placed, self.parts, self.sems = scratch
        self.count, self.cases = self.spread.shape
        self.tile = min(512, self.count)
        self.tiles = self.count // self.tile

    def rows(self, t):
        return pl.ds(pl.multiple_of(t * self.tile, self.tile), self.tile)

    def fetch(self, t):
        rows = self.rows(t)
        return pltpu.make_async_copy(self.matrix_hbm.at[rows], self.matrix.at[rows], self.sems.at[t])

    def start(self):
        @pl.loop(0, self.tiles)
        def _(t):
            self.fetch(t).start()

    def place(self):
        @pl.loop(0, self.tiles)
        def _(t):
            level = lax.broadcasted_iota(jnp.int32, (self.tile, self.count), 0) + t * self.tile
            select = (level == self.row_order[...]).astype(jnp.bfloat16)
            self.placed[self.rows(t), :] = jnp.dot(
                select, self.spread[...], preferred_element_type=jnp.float32
            ).astype(jnp.bfloat16)

    def multiply(self):
        @pl.loop(0, self.tiles)
        def _(t):
            self.fetch(t).wait()
            product = jnp.dot(
                self.matrix[self.rows(t), :], self.placed[...], preferred_element_type=jnp.float32
            )
            high = product.astype(jnp.bfloat16)
            self.parts[self.rows(t), : self.cases] = high
            self.parts[self.rows(t), self.cases :] = (product - high.astype(jnp.float32)).astype(jnp.bfloat16)

    def back(self, edge, mask):
        level = lax.broadcasted_iota(jnp.int32, (self.count // 4, self.count), 1)
        order = self.column_order[pl.ds(edge * (self.count // 4), self.count // 4), :]
        select = (level == order).astype(jnp.bfloat16)
        both = jnp.dot(select, self.parts[...], preferred_element_type=jnp.float32)
        held = over_cases(mask[pl.ds(edge, 1), :], self.cases)
        return (both[:, : self.cases] + both[:, self.cases :]) * held


def invert(factor, inverse):
    size = factor.shape[0]
    row = lax.broadcasted_iota(jnp.int32, (LANES, LANES), 0)
    column = lax.broadcasted_iota(jnp.int32, (LANES, LANES), 1)
    blocks = [pl.ds(at, LANES) for at in range(0, size, LANES)]

    def times(left, right):
        return jnp.dot(left, right, precision=HIGHEST, preferred_element_type=jnp.float32)

    inverse[...] = jnp.zeros((size, size), jnp.float32)
    corners = [factor[at, at] for at in blocks]
    solved = [jnp.where(row == column, 1.0 / corner, 0.0) for corner in corners]
    width = 1
    while width < LANES:
        joins = (row // (2 * width) == column // (2 * width)) & (row // width > column // width)
        half = [times(jnp.where(joins, c, 0.0), s) for c, s in zip(corners, solved)]
        solved = [s - times(s, h) for s, h in zip(solved, half)]
        width *= 2
    for n, at in enumerate(blocks):
        if n:
            before = pl.ds(0, n * LANES)
            inverse[at, before] = -times(solved[n], times(factor[at, before], inverse[before, before]))
        inverse[at, at] = solved[n]


def prepare_kernel(factor, piece_labels, corner_labels, couple, row_order, forward, backward, back, inverse):
    invert(factor, inverse)
    size, pieces = forward.shape
    level = lax.broadcasted_iota(jnp.int32, (size, pieces), 0)
    select = (level == piece_labels[...]).astype(jnp.float32)
    forward[...] = jnp.dot(inverse[...], select, precision=HIGHEST, preferred_element_type=jnp.float32)
    level = lax.broadcasted_iota(jnp.int32, backward.shape, 1)
    select = (level == corner_labels[...]).astype(jnp.float32)
    backward[...] = lax.dot_general(
        select, inverse[...], (((1,), (1,)), ((), ())), precision=HIGHEST, preferred_element_type=jnp.float32
    )
    count = couple.shape[1]
    tile = min(512, count)

    @pl.loop(0, count // tile)
    def _(t):
        at = pl.ds(pl.multiple_of(t * tile, tile), tile)
        level = lax.broadcasted_iota(jnp.int32, (count, tile), 0)
        select = (level == row_order[:, at]).astype(jnp.bfloat16)
        back[:, at] = jnp.dot(couple[...], select, preferred_element_type=jnp.float32)


def smooth_kernel(
    west, east, south, north, row_order, column_order, back, matrix_hbm,
    residual, west_out, east_out, south_out, north_out, total, mask, *scratch,
):
    block = Block(matrix_hbm, row_order, column_order, scratch)
    block.start()
    width, cases = block.count // 4, block.cases
    span = min(cases, width)
    messages = (west_out, east_out, south_out, north_out)
    for edge, (source, sign) in enumerate(((west, -1.0), (east, 1.0), (south, -1.0), (north, 1.0))):
        at = pl.ds(edge * width, width)
        residual[at, :] = sign * source[pl.ds(0, width), :]
        block.spread[at, :] = (0.5 * residual[at, :]).astype(jnp.bfloat16)
        for part in range(width // span):
            held = source[pl.ds(width + part, 1), :]
            mask[pl.ds(edge, 1), pl.ds(part * span, span)] = held
            messages[edge][pl.ds(width + part * CORNER_ROWS, CORNER_ROWS), :] = (
                back[:, pl.ds(edge * width + part * span, span)] * held
            )
    block.place()
    block.multiply()
    partial = jnp.zeros((1, cases), jnp.float32)
    for edge, message in enumerate(messages):
        sides = block.back(edge, mask)
        message[pl.ds(0, width), :] = sides
        partial += sum_rows(residual[pl.ds(edge * width, width), :] * sides)
    total[...] = jnp.broadcast_to(0.5 * partial, total.shape)


def apply_kernel(first, *refs):
    own, refs = refs[:4], refs[4:]
    received, refs = refs[:4], refs[4:]
    if first:
        (total,), refs = refs[:1], refs[1:]
    else:
        (old_direction, pieces, old_aligned), refs = refs[:3], refs[3:]
    row_order, column_order, mask, couple, matrix_hbm = refs[:5]
    direction, refs = refs[5], refs[6:]
    out, refs = refs[:4], refs[4:]
    copies, other = refs[:2]
    block = Block(matrix_hbm, row_order, column_order, refs[2:])
    block.start()
    count, cases = block.count, block.cases
    width = count // 4
    if not first:
        aligned = sum(pieces[device, 0:1, :] for device in range(pieces.shape[0]))
        ratio = aligned / old_aligned[0:1, :]
        other[...] = jnp.broadcast_to(aligned, other.shape)
    for edge in range(4):
        at = pl.ds(edge * width, width)
        smoothed = 0.5 * (own[edge][pl.ds(0, width), :] - received[edge][pl.ds(0, width), :])
        if not first:
            smoothed = smoothed + ratio * old_direction[at, :]
        direction[at, :] = smoothed
        block.spread[at, :] = smoothed.astype(jnp.bfloat16)
    block.place()
    block.multiply()
    curvature = jnp.zeros((1, cases), jnp.float32)
    for edge in range(4):
        at = pl.ds(edge * width, width)
        out[edge][...] = block.back(edge, mask)
        curvature += sum_rows(block.spread[at, :].astype(jnp.float32) * out[edge][...])
    terms = jnp.dot(couple[...], block.placed[...], preferred_element_type=jnp.float32)
    row = lax.broadcasted_iota(jnp.int32, (SUMS, cases), 0)
    sums = jnp.where(row == 0, curvature, 0.0)
    if first:
        sums = sums + jnp.where(row == 1, total[0:1, :], 0.0)
        cut = max(width // cases, 1)
        span = min(width, cases)
        for edge in range(4):
            for part in range(cut):
                at = pl.ds(edge * width + part * span, span)
                rows = pl.ds(width + part * CORNER_ROWS, CORNER_ROWS)
                other[pl.ds(0, CORNER_ROWS), at] = own[edge][rows, :]
                other[pl.ds(CORNER_ROWS, CORNER_ROWS), at] = -received[edge][rows, :]
    for device in range(copies.shape[0]):
        copies[device, pl.ds(0, CORNER_ROWS), :] = terms
        copies[device, pl.ds(CORNER_ROWS, SUMS), :] = sums


def strip_kernel(pieces, copies):
    devices, piece, cases = pieces.shape
    rows = copies.shape[1]
    half = 2 * (devices + 1)
    row = lax.broadcasted_iota(jnp.int32, (rows, devices * piece), 0)
    source = lax.broadcasted_iota(jnp.int32, (rows, devices * piece), 1)
    device, term = source // piece, source % piece
    target = (term // 2) % 2 * half + (device + term // 4) * 2 + term % 2
    target = jnp.where(term < CORNER_ROWS, target, 2 * half + term - CORNER_ROWS)
    select = (row == target).astype(jnp.float32)
    strip = jnp.dot(
        select,
        pieces[...].reshape(devices * piece, cases),
        precision=HIGHEST,
        preferred_element_type=jnp.float32,
    )
    for device in range(copies.shape[0]):
        copies[device] = strip


def update_kernel(first, last, *refs):
    pieces, forward, backward, edge_couple, direction, residual_in = refs[:6]
    own, refs = refs[6:10], refs[10:]
    received, refs = refs[:4], refs[4:]
    if not first:
        (multipliers_in, old_aligned), refs = refs[:2], refs[2:]
    row_order, column_order, mask, matrix_hbm = refs[:4]
    residual, multipliers = refs[4:6]
    out, refs = refs[6:10], refs[10:]
    copies = refs[0]
    if first:
        aligned_out, refs = refs[1], refs[2:]
    else:
        refs = refs[1:]
    kept, *scratch = refs
    block = Block(matrix_hbm, row_order, column_order, scratch)
    block.start()
    count, cases = block.count, block.cases
    width = count // 4
    devices, piece, _ = pieces.shape
    scalar_row = piece - SUMS // 2
    sums = sum(pieces[device, pl.ds(scalar_row, SUMS // 2), :] for device in range(devices))
    half_solved = jnp.dot(
        forward[...],
        pieces[...].reshape(devices * piece, cases),
        precision=HIGHEST,
        preferred_element_type=jnp.float32,
    )
    corners = jnp.dot(backward[...], half_solved, precision=HIGHEST, preferred_element_type=jnp.float32)
    curvature = sums[0:1, :] + sum_rows(half_solved * half_solved)
    if first:
        aligned = sums[1:2, :]
        aligned_out[...] = jnp.broadcast_to(aligned, aligned_out.shape)
    else:
        aligned = old_aligned[0:1, :]
    step_size = aligned / curvature
    for edge in range(4):
        at = pl.ds(edge * width, width)
        beyond = pl.ds((edge + 1) * CORNER_ROWS, CORNER_ROWS)
        solved = jnp.concatenate(
            [corners[0:CORNER_ROWS], corners[(edge + 1) * CORNER_ROWS : (edge + 2) * CORNER_ROWS]]
        )
        high = solved.astype(jnp.bfloat16)
        rest = solved - high.astype(jnp.float32)
        middle = rest.astype(jnp.bfloat16)
        low = (rest - middle.astype(jnp.float32)).astype(jnp.bfloat16)
        coupling = edge_couple[:, at].astype(jnp.bfloat16)
        coarse = lax.dot_general(
            jnp.concatenate([coupling] * 3),
            jnp.concatenate([high, middle, low]),
            (((0,), (0,)), ((), ())),
            preferred_element_type=jnp.float32,
        )
        image = own[edge][...] - received[edge][...] + coarse
        updated = residual_in[at, :] - step_size * image
        block.spread[at, :] = (0.5 * updated).astype(jnp.bfloat16)
        if last:
            kept[at, :] = updated
            if edge % 2:
                residual[edge // 2] = updated
                multipliers[edge // 2] = multipliers_in[at, :] + step_size * direction[at, :]
        else:
            residual[at, :] = updated
            multipliers[at, :] = step_size * direction[at, :]
    block.place()
    block.multiply()
    partial = jnp.zeros((1, cases), jnp.float32)
    current = kept if last else residual
    for edge in range(4):
        out[edge][...] = block.back(edge, mask)
        partial += sum_rows(current[pl.ds(edge * width, width), :] * out[edge][...])
    copies[...] = jnp.broadcast_to(0.5 * partial, copies.shape)


def add_kernel(pieces, copies):
    copies[...] = jnp.broadcast_to(sum(pieces[device] for device in range(pieces.shape[0])), copies.shape)


def finish_kernel(east, north, from_east, from_north, old_direction, pieces, old_aligned, direction):
    width = east.shape[0]
    ratio = sum(pieces[device, 0:1, :] for device in range(pieces.shape[0])) / old_aligned[0:1, :]
    for at, own, received, old in ((0, east, from_east, width), (1, north, from_north, 3 * width)):
        direction[at] = 0.5 * (own[...] - received[...]) + ratio * old_direction[pl.ds(old, width), :]


def piece_cross_labels(corner_map):
    columns, rows, corners = corner_map.shape
    fields = corners // 4

    def corner(at, rows_of):
        return corner_map[:, rows_of, at * fields : (at + 1) * fields]

    sides = [
        jnp.concatenate([corner(east, slice(None)), corner(2 + east, slice(rows - 1, rows))], axis=1)
        for east in range(2)
    ]
    strips = jnp.concatenate([side.reshape(columns, -1) for side in sides], axis=1)
    none = jnp.full((columns, SUMS // 2), -1, corner_map.dtype)
    return jnp.concatenate([strips, none], axis=1).reshape(1, -1)


def body(load_jump, flex, precond, couple, edge_map, flags, corner_map, coarse_factor):
    _, width, cases = load_jump.shape[2:]
    count = 4 * width
    order = edge_map[0, 0]
    flex_local = flex[0, 0]
    precond_local = precond[0, 0]
    couple_local = couple[0, 0]
    column_index = lax.axis_index("gx")
    row_index = lax.axis_index("gy")
    columns = lax.axis_size("gx")
    rows = lax.axis_size("gy")
    coarse_count = coarse_factor.shape[0]
    coarse_size = -(-coarse_count // LANES) * LANES
    strip_rows = 4 * (rows + 1) + SUMS // 2

    inside = jnp.stack([column_index < columns - 1, row_index < rows - 1]).astype(jnp.float32)
    live = flags[0, 0].astype(jnp.float32) * inside[:, None]
    mask_rows = max(width // cases, 1)
    held = jnp.pad(live.reshape(2, mask_rows, -1), ((0, 0), (0, 8 - mask_rows), (0, 0)))
    own = jnp.concatenate([live[:, :, None] * load_jump[0, 0], held], axis=1)
    east, north = own[0], own[1]
    west = shift(east, "gx", 1)
    south = shift(north, "gy", 1)

    piece_labels = piece_cross_labels(corner_map)
    around = jnp.concatenate(
        [
            lax.dynamic_slice(
                corner_map,
                (
                    jnp.clip(column_index + dx, 0, columns - 1),
                    jnp.clip(row_index + dy, 0, rows - 1),
                    0,
                ),
                (1, 1, CORNER_ROWS),
            ).reshape(-1, 1)
            for dx, dy in ((0, 0), (-1, 0), (1, 0), (0, -1), (0, 1))
        ]
    )
    spare = coarse_size - coarse_count
    levels = lax.iota(jnp.int32, coarse_size)
    factor = jnp.pad(coarse_factor, ((0, spare), (0, spare))) + jnp.where(
        (levels[:, None] == levels[None, :]) & (levels[:, None] >= coarse_count), 1.0, 0.0
    )
    forward, backward, back = call(
        prepare_kernel,
        (
            shaped(coarse_size, columns * strip_rows),
            shaped(5 * CORNER_ROWS, coarse_size),
            shaped(CORNER_ROWS, count),
        ),
        (factor, piece_labels, around, couple_local, order[None, :]),
        [pltpu.VMEM((coarse_size, coarse_size), jnp.float32)],
        flops=10**10,
    )

    row_order = order[None, :]
    column_order = order[:, None]
    scratch = block_scratch(count, cases)
    block_flops = 8 * count * count * cases
    message = shaped(width + CORNER_ROWS * max(width // cases, 1), cases)
    edge = shaped(width, cases)
    whole = shaped(count, cases)
    row = shaped(8, cases)

    residual, *sides, total, mask = call(
        smooth_kernel,
        (whole, message, message, message, message, row, shaped(4, width)),
        (west, east, south, north, row_order, column_order, back, precond_local),
        scratch,
        in_hbm=(7,),
        flops=block_flops,
    )
    received = exchange(*sides)
    multipliers = aligned = direction = pieces = edge_couple = None
    for iteration in range(ITERS):
        first = iteration == 0
        last = iteration == ITERS - 1
        beside = (total,) if first else (direction, pieces, aligned)
        operands = (*sides, *received, *beside, row_order, column_order, mask, couple_local, flex_local)
        direction, *sides, copies, other = call(
            functools.partial(apply_kernel, first),
            (
                whole, edge, edge, edge, edge,
                shaped(rows, CORNER_ROWS + SUMS, cases),
                shaped(2 * CORNER_ROWS, count) if first else row,
            ),
            operands,
            scratch,
            in_hbm=(len(operands) - 1,),
            flops=block_flops,
        )
        if first:
            edge_couple = other
        else:
            aligned = other
        received, copies = lax.optimization_barrier((exchange(*sides), copies))
        strips = call(strip_kernel, shaped(columns, strip_rows, cases), (swap(copies, "gy"),))
        pieces = swap(strips, "gx")
        operands = (pieces, forward, backward, edge_couple, direction, residual, *sides, *received)
        if not first:
            operands += (multipliers, aligned)
        operands += (row_order, column_order, mask, precond_local)
        kept = shaped(2, width, cases) if last else whole
        residual, multipliers, *sides = call(
            functools.partial(update_kernel, first, last),
            (kept, kept, edge, edge, edge, edge, shaped(rows, 8, cases)) + ((row,) if first else ()),
            operands,
            [pltpu.VMEM((count, cases), jnp.float32) if last else pltpu.VMEM((8, LANES), jnp.float32)]
            + scratch,
            in_hbm=(len(operands) - 1,),
            flops=block_flops,
            limit=57,
        )
        if first:
            *sides, copies, aligned = sides
        else:
            *sides, copies = sides
        if last:
            from_east = shift(sides[0], "gx", -1)
            from_north = shift(sides[2], "gy", -1)
        else:
            received = exchange(*sides)
        pieces = swap(call(add_kernel, shaped(columns, 8, cases), (swap(copies, "gy"),)), "gx")
    direction = call(
        finish_kernel,
        shaped(2, width, cases),
        (sides[1], sides[3], from_east, from_north, direction, pieces, aligned),
    )
    return multipliers[None, None], residual[None, None], direction[None, None]


def solution(mesh):
    return jax.shard_map(
        body,
        mesh=mesh,
        in_specs=(
            P("gx", "gy", None, None, None),
            P("gx", "gy", None, None),
            P("gx", "gy", None, None),
            P("gx", "gy", None, None),
            P("gx", "gy", None),
            P("gx", "gy", None, None),
            P(),
            P(),
        ),
        out_specs=(
            P("gx", "gy", None, None, None),
            P("gx", "gy", None, None, None),
            P("gx", "gy", None, None, None),
        ),
        check_vma=False,
    )
```

```python
import functools

import jax
import jax.numpy as jnp
from jax import lax
from jax.experimental import pallas as pl
from jax.experimental.pallas import tpu as pltpu
from jax.sharding import PartitionSpec as P

ITERS = 2
HIGHEST = lax.Precision.HIGHEST
LANES = 128
CORNER_ROWS = 8
SUMS = 8


def shift(shard, axis, by):
    devices = lax.axis_size(axis)
    pairs = [(i, i + by) for i in range(devices) if 0 <= i + by < devices]
    return lax.ppermute(shard, axis, pairs)


def exchange(west, east, south, north):
    return shift(east, "gx", 1), shift(west, "gx", -1), shift(north, "gy", 1), shift(south, "gy", -1)


def swap(copies, axis):
    return lax.all_to_all(copies, axis, 0, 0, tiled=True)


def call(kernel, out_shape, operands, scratch_shapes=(), in_hbm=(), flops=0, limit=46):
    vmem = pl.BlockSpec(memory_space=pltpu.VMEM)
    specs = [
        pl.BlockSpec(memory_space=pl.ANY) if at in in_hbm else vmem for at in range(len(operands))
    ]
    moved = sum(a.size * a.dtype.itemsize for a in operands)
    return pl.pallas_call(
        kernel,
        out_shape=out_shape,
        in_specs=specs,
        out_specs=jax.tree.map(lambda _: vmem, out_shape),
        scratch_shapes=list(scratch_shapes),
        compiler_params=pltpu.CompilerParams(vmem_limit_bytes=limit * 2**20),
        cost_estimate=pl.CostEstimate(flops=flops, bytes_accessed=moved, transcendentals=0),
    )(*operands)


def shaped(*shape, dtype=jnp.float32):
    return jax.ShapeDtypeStruct(shape, dtype)


def sum_rows(values):
    return jnp.sum(values, axis=0, keepdims=True)


def over_cases(row, cases):
    first = lax.broadcasted_iota(jnp.int32, (16, row.shape[1]), 0) == 0
    rows = jnp.where(first, jnp.broadcast_to(row, first.shape), 0.0).astype(jnp.bfloat16)
    ones = jnp.ones((16, cases), jnp.bfloat16)
    return lax.dot_general(rows, ones, (((0,), (0,)), ((), ())), preferred_element_type=jnp.float32)


def block_scratch(count, cases):
    tile = min(512, count)
    return [
        pltpu.VMEM((count, count), jnp.bfloat16),
        pltpu.VMEM((count, cases), jnp.bfloat16),
        pltpu.VMEM((count, cases), jnp.bfloat16),
        pltpu.VMEM((count, 2 * cases), jnp.bfloat16),
        pltpu.SemaphoreType.DMA((count // tile,)),
    ]


class Block:
    def __init__(self, matrix_hbm, row_order, column_order, scratch):
        self.matrix_hbm = matrix_hbm
        self.row_order = row_order
        self.column_order = column_order
        self.matrix, self.spread, self.placed, self.parts, self.sems = scratch
        self.count, self.cases = self.spread.shape
        self.tile = min(512, self.count)
        self.tiles = self.count // self.tile

    def rows(self, t):
        return pl.ds(pl.multiple_of(t * self.tile, self.tile), self.tile)

    def fetch(self, t):
        rows = self.rows(t)
        return pltpu.make_async_copy(self.matrix_hbm.at[rows], self.matrix.at[rows], self.sems.at[t])

    def start(self):
        @pl.loop(0, self.tiles)
        def _(t):
            self.fetch(t).start()

    def place(self):
        @pl.loop(0, self.tiles)
        def _(t):
            level = lax.broadcasted_iota(jnp.int32, (self.tile, self.count), 0) + t * self.tile
            select = (level == self.row_order[...]).astype(jnp.bfloat16)
            self.placed[self.rows(t), :] = jnp.dot(
                select, self.spread[...], preferred_element_type=jnp.float32
            ).astype(jnp.bfloat16)

    def multiply(self):
        @pl.loop(0, self.tiles)
        def _(t):
            self.fetch(t).wait()
            product = jnp.dot(
                self.matrix[self.rows(t), :], self.placed[...], preferred_element_type=jnp.float32
            )
            high = product.astype(jnp.bfloat16)
            self.parts[self.rows(t), : self.cases] = high
            self.parts[self.rows(t), self.cases :] = (product - high.astype(jnp.float32)).astype(jnp.bfloat16)

    def back(self, edge, mask):
        level = lax.broadcasted_iota(jnp.int32, (self.count // 4, self.count), 1)
        order = self.column_order[pl.ds(edge * (self.count // 4), self.count // 4), :]
        select = (level == order).astype(jnp.bfloat16)
        both = jnp.dot(select, self.parts[...], preferred_element_type=jnp.float32)
        held = over_cases(mask[pl.ds(edge, 1), :], self.cases)
        return (both[:, : self.cases] + both[:, self.cases :]) * held


def invert(factor, inverse):
    size = factor.shape[0]
    row = lax.broadcasted_iota(jnp.int32, (LANES, LANES), 0)
    column = lax.broadcasted_iota(jnp.int32, (LANES, LANES), 1)
    blocks = [pl.ds(at, LANES) for at in range(0, size, LANES)]

    def times(left, right):
        return jnp.dot(left, right, precision=HIGHEST, preferred_element_type=jnp.float32)

    inverse[...] = jnp.zeros((size, size), jnp.float32)
    corners = [factor[at, at] for at in blocks]
    solved = [jnp.where(row == column, 1.0 / corner, 0.0) for corner in corners]
    width = 1
    while width < LANES:
        joins = (row // (2 * width) == column // (2 * width)) & (row // width > column // width)
        half = [times(jnp.where(joins, c, 0.0), s) for c, s in zip(corners, solved)]
        solved = [s - times(s, h) for s, h in zip(solved, half)]
        width *= 2
    for n, at in enumerate(blocks):
        if n:
            before = pl.ds(0, n * LANES)
            inverse[at, before] = -times(solved[n], times(factor[at, before], inverse[before, before]))
        inverse[at, at] = solved[n]


def prepare_kernel(factor, piece_labels, corner_labels, couple, row_order, forward, backward, back, inverse):
    invert(factor, inverse)
    size, pieces = forward.shape
    level = lax.broadcasted_iota(jnp.int32, (size, pieces), 0)
    select = (level == piece_labels[...]).astype(jnp.float32)
    forward[...] = jnp.dot(inverse[...], select, precision=HIGHEST, preferred_element_type=jnp.float32)
    level = lax.broadcasted_iota(jnp.int32, backward.shape, 1)
    select = (level == corner_labels[...]).astype(jnp.float32)
    backward[...] = lax.dot_general(
        select, inverse[...], (((1,), (1,)), ((), ())), precision=HIGHEST, preferred_element_type=jnp.float32
    )
    count = couple.shape[1]
    tile = min(512, count)

    @pl.loop(0, count // tile)
    def _(t):
        at = pl.ds(pl.multiple_of(t * tile, tile), tile)
        level = lax.broadcasted_iota(jnp.int32, (count, tile), 0)
        select = (level == row_order[:, at]).astype(jnp.bfloat16)
        back[:, at] = jnp.dot(couple[...], select, preferred_element_type=jnp.float32)


def smooth_kernel(
    west, east, south, north, row_order, column_order, back, matrix_hbm,
    residual, west_out, east_out, south_out, north_out, total, mask, *scratch,
):
    block = Block(matrix_hbm, row_order, column_order, scratch)
    block.start()
    width, cases = block.count // 4, block.cases
    span = min(cases, width)
    messages = (west_out, east_out, south_out, north_out)
    for edge, (source, sign) in enumerate(((west, -1.0), (east, 1.0), (south, -1.0), (north, 1.0))):
        at = pl.ds(edge * width, width)
        residual[at, :] = sign * source[pl.ds(0, width), :]
        block.spread[at, :] = (0.5 * residual[at, :]).astype(jnp.bfloat16)
        for part in range(width // span):
            held = source[pl.ds(width + part, 1), :]
            mask[pl.ds(edge, 1), pl.ds(part * span, span)] = held
            messages[edge][pl.ds(width + part * CORNER_ROWS, CORNER_ROWS), :] = (
                back[:, pl.ds(edge * width + part * span, span)] * held
            )
    block.place()
    block.multiply()
    partial = jnp.zeros((1, cases), jnp.float32)
    for edge, message in enumerate(messages):
        sides = block.back(edge, mask)
        message[pl.ds(0, width), :] = sides
        partial += sum_rows(residual[pl.ds(edge * width, width), :] * sides)
    total[...] = jnp.broadcast_to(0.5 * partial, total.shape)


def apply_kernel(first, *refs):
    own, refs = refs[:4], refs[4:]
    received, refs = refs[:4], refs[4:]
    if first:
        (total,), refs = refs[:1], refs[1:]
    else:
        (old_direction, pieces, old_aligned), refs = refs[:3], refs[3:]
    row_order, column_order, mask, couple, matrix_hbm = refs[:5]
    direction, refs = refs[5], refs[6:]
    out, refs = refs[:4], refs[4:]
    copies, other = refs[:2]
    block = Block(matrix_hbm, row_order, column_order, refs[2:])
    block.start()
    count, cases = block.count, block.cases
    width = count // 4
    if not first:
        aligned = sum(pieces[device, 0:1, :] for device in range(pieces.shape[0]))
        ratio = aligned / old_aligned[0:1, :]
        other[...] = jnp.broadcast_to(aligned, other.shape)
    for edge in range(4):
        at = pl.ds(edge * width, width)
        smoothed = 0.5 * (own[edge][pl.ds(0, width), :] - received[edge][pl.ds(0, width), :])
        if not first:
            smoothed = smoothed + ratio * old_direction[at, :]
        direction[at, :] = smoothed
        block.spread[at, :] = smoothed.astype(jnp.bfloat16)
    block.place()
    block.multiply()
    curvature = jnp.zeros((1, cases), jnp.float32)
    for edge in range(4):
        at = pl.ds(edge * width, width)
        out[edge][...] = block.back(edge, mask)
        curvature += sum_rows(block.spread[at, :].astype(jnp.float32) * out[edge][...])
    terms = jnp.dot(couple[...], block.placed[...], preferred_element_type=jnp.float32)
    row = lax.broadcasted_iota(jnp.int32, (SUMS, cases), 0)
    sums = jnp.where(row == 0, curvature, 0.0)
    if first:
        sums = sums + jnp.where(row == 1, total[0:1, :], 0.0)
        cut = max(width // cases, 1)
        span = min(width, cases)
        for edge in range(4):
            for part in range(cut):
                at = pl.ds(edge * width + part * span, span)
                rows = pl.ds(width + part * CORNER_ROWS, CORNER_ROWS)
                other[pl.ds(0, CORNER_ROWS), at] = own[edge][rows, :]
                other[pl.ds(CORNER_ROWS, CORNER_ROWS), at] = -received[edge][rows, :]
    for device in range(copies.shape[0]):
        copies[device, pl.ds(0, CORNER_ROWS), :] = terms
        copies[device, pl.ds(CORNER_ROWS, SUMS), :] = sums


def strip_kernel(pieces, copies):
    devices, piece, cases = pieces.shape
    rows = copies.shape[1]
    half = 2 * (devices + 1)
    row = lax.broadcasted_iota(jnp.int32, (rows, devices * piece), 0)
    source = lax.broadcasted_iota(jnp.int32, (rows, devices * piece), 1)
    device, term = source // piece, source % piece
    target = (term // 2) % 2 * half + (device + term // 4) * 2 + term % 2
    target = jnp.where(term < CORNER_ROWS, target, 2 * half + term - CORNER_ROWS)
    select = (row == target).astype(jnp.float32)
    strip = jnp.dot(
        select,
        pieces[...].reshape(devices * piece, cases),
        precision=HIGHEST,
        preferred_element_type=jnp.float32,
    )
    for device in range(copies.shape[0]):
        copies[device] = strip


def update_kernel(first, last, *refs):
    pieces, forward, backward, edge_couple, direction, residual_in = refs[:6]
    own, refs = refs[6:10], refs[10:]
    received, refs = refs[:4], refs[4:]
    if not first:
        (multipliers_in, old_aligned), refs = refs[:2], refs[2:]
    row_order, column_order, mask, matrix_hbm = refs[:4]
    residual, multipliers = refs[4:6]
    out, refs = refs[6:10], refs[10:]
    copies = refs[0]
    if first:
        aligned_out, refs = refs[1], refs[2:]
    else:
        refs = refs[1:]
    kept, *scratch = refs
    block = Block(matrix_hbm, row_order, column_order, scratch)
    block.start()
    count, cases = block.count, block.cases
    width = count // 4
    devices, piece, _ = pieces.shape
    scalar_row = piece - SUMS // 2
    sums = sum(pieces[device, pl.ds(scalar_row, SUMS // 2), :] for device in range(devices))
    half_solved = jnp.dot(
        forward[...],
        pieces[...].reshape(devices * piece, cases),
        precision=HIGHEST,
        preferred_element_type=jnp.float32,
    )
    corners = jnp.dot(backward[...], half_solved, precision=HIGHEST, preferred_element_type=jnp.float32)
    curvature = sums[0:1, :] + sum_rows(half_solved * half_solved)
    if first:
        aligned = sums[1:2, :]
        aligned_out[...] = jnp.broadcast_to(aligned, aligned_out.shape)
    else:
        aligned = old_aligned[0:1, :]
    step_size = aligned / curvature
    for edge in range(4):
        at = pl.ds(edge * width, width)
        beyond = pl.ds((edge + 1) * CORNER_ROWS, CORNER_ROWS)
        solved = jnp.concatenate(
            [corners[0:CORNER_ROWS], corners[(edge + 1) * CORNER_ROWS : (edge + 2) * CORNER_ROWS]]
        )
        high = solved.astype(jnp.bfloat16)
        rest = solved - high.astype(jnp.float32)
        middle = rest.astype(jnp.bfloat16)
        low = (rest - middle.astype(jnp.float32)).astype(jnp.bfloat16)
        coupling = edge_couple[:, at].astype(jnp.bfloat16)
        coarse = lax.dot_general(
            jnp.concatenate([coupling] * 3),
            jnp.concatenate([high, middle, low]),
            (((0,), (0,)), ((), ())),
            preferred_element_type=jnp.float32,
        )
        image = own[edge][...] - received[edge][...] + coarse
        updated = residual_in[at, :] - step_size * image
        block.spread[at, :] = (0.5 * updated).astype(jnp.bfloat16)
        if last:
            kept[at, :] = updated
            if edge % 2:
                residual[edge // 2] = updated
                multipliers[edge // 2] = multipliers_in[at, :] + step_size * direction[at, :]
        else:
            residual[at, :] = updated
            multipliers[at, :] = step_size * direction[at, :]
    block.place()
    block.multiply()
    partial = jnp.zeros((1, cases), jnp.float32)
    current = kept if last else residual
    for edge in range(4):
        out[edge][...] = block.back(edge, mask)
        partial += sum_rows(current[pl.ds(edge * width, width), :] * out[edge][...])
    copies[...] = jnp.broadcast_to(0.5 * partial, copies.shape)


def add_kernel(pieces, copies):
    copies[...] = jnp.broadcast_to(sum(pieces[device] for device in range(pieces.shape[0])), copies.shape)


def finish_kernel(east, north, from_east, from_north, old_direction, pieces, old_aligned, direction):
    width = east.shape[0]
    ratio = sum(pieces[device, 0:1, :] for device in range(pieces.shape[0])) / old_aligned[0:1, :]
    for at, own, received, old in ((0, east, from_east, width), (1, north, from_north, 3 * width)):
        direction[at] = 0.5 * (own[...] - received[...]) + ratio * old_direction[pl.ds(old, width), :]


def piece_cross_labels(corner_map):
    columns, rows, corners = corner_map.shape
    fields = corners // 4

    def corner(at, rows_of):
        return corner_map[:, rows_of, at * fields : (at + 1) * fields]

    sides = [
        jnp.concatenate([corner(east, slice(None)), corner(2 + east, slice(rows - 1, rows))], axis=1)
        for east in range(2)
    ]
    strips = jnp.concatenate([side.reshape(columns, -1) for side in sides], axis=1)
    none = jnp.full((columns, SUMS // 2), -1, corner_map.dtype)
    return jnp.concatenate([strips, none], axis=1).reshape(1, -1)


def body(load_jump, flex, precond, couple, edge_map, flags, corner_map, coarse_factor):
    _, width, cases = load_jump.shape[2:]
    count = 4 * width
    order = edge_map[0, 0]
    flex_local = flex[0, 0]
    precond_local = precond[0, 0]
    couple_local = couple[0, 0]
    column_index = lax.axis_index("gx")
    row_index = lax.axis_index("gy")
    columns = lax.axis_size("gx")
    rows = lax.axis_size("gy")
    coarse_count = coarse_factor.shape[0]
    coarse_size = -(-coarse_count // LANES) * LANES
    strip_rows = 4 * (rows + 1) + SUMS // 2

    inside = jnp.stack([column_index < columns - 1, row_index < rows - 1]).astype(jnp.float32)
    live = flags[0, 0].astype(jnp.float32) * inside[:, None]
    mask_rows = max(width // cases, 1)
    held = jnp.pad(live.reshape(2, mask_rows, -1), ((0, 0), (0, 8 - mask_rows), (0, 0)))
    own = jnp.concatenate([live[:, :, None] * load_jump[0, 0], held], axis=1)
    east, north = own[0], own[1]
    west = shift(east, "gx", 1)
    south = shift(north, "gy", 1)

    piece_labels = piece_cross_labels(corner_map)
    around = jnp.concatenate(
        [
            lax.dynamic_slice(
                corner_map,
                (
                    jnp.clip(column_index + dx, 0, columns - 1),
                    jnp.clip(row_index + dy, 0, rows - 1),
                    0,
                ),
                (1, 1, CORNER_ROWS),
            ).reshape(-1, 1)
            for dx, dy in ((0, 0), (-1, 0), (1, 0), (0, -1), (0, 1))
        ]
    )
    spare = coarse_size - coarse_count
    levels = lax.iota(jnp.int32, coarse_size)
    factor = jnp.pad(coarse_factor, ((0, spare), (0, spare))) + jnp.where(
        (levels[:, None] == levels[None, :]) & (levels[:, None] >= coarse_count), 1.0, 0.0
    )
    forward, backward, back = call(
        prepare_kernel,
        (
            shaped(coarse_size, columns * strip_rows),
            shaped(5 * CORNER_ROWS, coarse_size),
            shaped(CORNER_ROWS, count),
        ),
        (factor, piece_labels, around, couple_local, order[None, :]),
        [pltpu.VMEM((coarse_size, coarse_size), jnp.float32)],
        flops=10**10,
    )

    row_order = order[None, :]
    column_order = order[:, None]
    scratch = block_scratch(count, cases)
    block_flops = 8 * count * count * cases
    message = shaped(width + CORNER_ROWS * max(width // cases, 1), cases)
    edge = shaped(width, cases)
    whole = shaped(count, cases)
    row = shaped(8, cases)

    residual, *sides, total, mask = call(
        smooth_kernel,
        (whole, message, message, message, message, row, shaped(4, width)),
        (west, east, south, north, row_order, column_order, back, precond_local),
        scratch,
        in_hbm=(7,),
        flops=block_flops,
    )
    received = exchange(*sides)
    multipliers = aligned = direction = pieces = edge_couple = None
    for iteration in range(ITERS):
        first = iteration == 0
        last = iteration == ITERS - 1
        beside = (total,) if first else (direction, pieces, aligned)
        operands = (*sides, *received, *beside, row_order, column_order, mask, couple_local, flex_local)
        direction, *sides, copies, other = call(
            functools.partial(apply_kernel, first),
            (
                whole, edge, edge, edge, edge,
                shaped(rows, CORNER_ROWS + SUMS, cases),
                shaped(2 * CORNER_ROWS, count) if first else row,
            ),
            operands,
            scratch,
            in_hbm=(len(operands) - 1,),
            flops=block_flops,
            limit=46 if first else 57,
        )
        if first:
            edge_couple = other
        else:
            aligned = other
        received = exchange(*sides)
        strips = call(strip_kernel, shaped(columns, strip_rows, cases), (swap(copies, "gy"),))
        pieces = swap(strips, "gx")
        operands = (pieces, forward, backward, edge_couple, direction, residual, *sides, *received)
        if not first:
            operands += (multipliers, aligned)
        operands += (row_order, column_order, mask, precond_local)
        kept = shaped(2, width, cases) if last else whole
        residual, multipliers, *sides = call(
            functools.partial(update_kernel, first, last),
            (kept, kept, edge, edge, edge, edge, shaped(rows, 8, cases)) + ((row,) if first else ()),
            operands,
            [pltpu.VMEM((count, cases), jnp.float32) if last else pltpu.VMEM((8, LANES), jnp.float32)]
            + scratch,
            in_hbm=(len(operands) - 1,),
            flops=block_flops,
            limit=57,
        )
        if first:
            *sides, copies, aligned = sides
        else:
            *sides, copies = sides
        if last:
            from_east = shift(sides[0], "gx", -1)
            from_north = shift(sides[2], "gy", -1)
        else:
            received = exchange(*sides)
        pieces = swap(call(add_kernel, shaped(columns, 8, cases), (swap(copies, "gy"),)), "gx")
    direction = call(
        finish_kernel,
        shaped(2, width, cases),
        (sides[1], sides[3], from_east, from_north, direction, pieces, aligned),
        limit=57,
    )
    return multipliers[None, None], residual[None, None], direction[None, None]


def solution(mesh):
    return jax.shard_map(
        body,
        mesh=mesh,
        in_specs=(
            P("gx", "gy", None, None, None),
            P("gx", "gy", None, None),
            P("gx", "gy", None, None),
            P("gx", "gy", None, None),
            P("gx", "gy", None),
            P("gx", "gy", None, None),
            P(),
            P(),
        ),
        out_specs=(
            P("gx", "gy", None, None, None),
            P("gx", "gy", None, None, None),
            P("gx", "gy", None, None, None),
        ),
        check_vma=False,
    )
```
